128 devices in a mesh: replica: 16 (over x, y_lo, core), expert: 4 (over z), tensor: 2 (over y_hi).
Axes of the slice: x: 4, y: 4 (y_hi: 2, y_lo: 2; y = y_hi * 2 + y_lo), z: 4, core: 2. Of those that a mesh axis runs over, the one named last changes fastest.
Arguments:
- kv_param: float32 [4, 64, 128, 128], P('tensor', ('replica', 'expert')), may hold values from -60 to 60, as said below
- kv_grad: float32 [4, 64, 128, 128], P('tensor', ('replica', 'expert')), as said below
- kv_mean: float32 [4, 64, 128, 128], P('tensor', ('replica', 'expert')), as said below
- kv_square: float32 [4, 64, 128, 128], P('tensor', ('replica', 'expert')), as said below
- exp_param: float32 [4, 2, 192, 128, 128], P(None, 'tensor', ('replica', 'expert')), may hold values from -60 to 60, as said below
- exp_grad: float32 [4, 2, 192, 128, 128], P(None, 'tensor', ('replica', 'expert')), as said below
- exp_mean: float32 [4, 2, 192, 128, 128], P(None, 'tensor', ('replica', 'expert')), as said below
- exp_square: float32 [4, 2, 192, 128, 128], P(None, 'tensor', ('replica', 'expert')), as said below
- expert_owner: int32 [4], replicated, may hold values from 0 to 3, as said below
Outputs:
- kv_param_new: float32 [4, 64, 128, 128], P('tensor', ('replica', 'expert'))
- exp_param_new: float32 [4, 2, 192, 128, 128], P(None, 'tensor', ('replica', 'expert'))
- kv_rollout: bfloat16 [4, 64, 128, 128], P('tensor')
- kv_scales: float32 [4, 64], P('tensor')
- exp_rollout: bfloat16 [8, 2, 192, 128, 128], P('expert', 'tensor')
- exp_scales: float32 [8, 2, 192], P('expert', 'tensor')
The draws below stay inside these ranges and needn't reach their ends.
Inputs may be any that keep to these rules, and one draw needn't show every extreme that they name: `expert_owner`: each of the 4 rollout expert shards owns at most 2 experts; in every draw one shard owns exactly 2. `kv_param`: master blocks of order one. `exp_param`: master blocks of order one. `kv_grad`: gradient entries of order one over the square root of the parameter count, give or take a factor of ten. `exp_grad`: gradient entries of order one over the square root of the parameter count, give or take a factor of ten. `kv_mean`: first moments of the gradients' order. `exp_mean`: first moments of the gradients' order. `kv_square`: positive second moments. `exp_square`: positive second moments.
All inputs are finite; a program needn't handle non-finite values. Where the reference program divides by a largest or mean magnitude, that divisor is 1e-20 or more.
Results may differ from the reference program's by a relative error of at most 0.001.
The reference program's roundings to bfloat16 on the way count: a program that leaves them out, or rounds other values in their place, can miss the bound.
Values may be sent and summed in bfloat16 or wider, within the bound.
No kernel may reach another device: no remote copies, remote signals or barrier semaphores. Data moves between devices by JAX's collectives and lax.ppermute only.
A program may use at most 192 MiB of HBM per device.

```python
import jax
import jax.numpy as jnp
from jax import lax

D = 4096
KVW = 512
FF = 1536
BLK = 128
SLOTS = 2
EXPERTS = 4
KV_COLB = 4
KV_ROWB = 64
EXP_BLK = 192
N_EXPERT = 4
N_TENSOR = 2


def rough_field(key, shape):
    field = jnp.clip(jax.random.normal(key, shape, jnp.float32), -6.0, 6.0)
    return field


def rising(shape, along):
    length = shape[along]
    fraction = jnp.arange(length, dtype=jnp.float32) / max(length - 1, 1)
    view = [1] * len(shape)
    view[along] = length
    return jnp.exp(fraction * 1.0986123).reshape(view)


def grad_scale():
    return float(2 * D * KVW + EXPERTS * FF * D) ** (-0.5)


def block_factor(key, shape):
    spread = jax.random.uniform(key, shape[:-2] + (1, 1), jnp.float32, -2.3, 2.3)
    return 0.3043 * jnp.exp(spread)


def param_field(key, shape):
    base_key = jax.random.fold_in(key, 0)
    field = rough_field(base_key, shape)
    return field


def gradient_field(key, shape, along):
    base_key = jax.random.fold_in(key, 0)
    factor_key = jax.random.fold_in(key, 2)
    field = rough_field(base_key, shape)
    return field * block_factor(factor_key, shape) * rising(shape, along) * grad_scale()


def mean_field(key, shape):
    return 0.2 * grad_scale() * rough_field(key, shape)


def square_field(key, shape):
    spread = jax.random.uniform(key, shape, jnp.float32, -2.9957323, -0.6931472)
    return grad_scale() * grad_scale() * jnp.exp(spread)


def kv_shape():
    return (KV_COLB, KV_ROWB, BLK, BLK)


def exp_shape():
    return (EXPERTS, N_TENSOR, EXP_BLK, BLK, BLK)


def draw_kv_param(key, part):
    return param_field(jax.random.fold_in(key, 101), kv_shape())


def draw_kv_grad(key, part):
    return gradient_field(jax.random.fold_in(key, 102), kv_shape(), 1)


def draw_kv_mean(key, part):
    return mean_field(jax.random.fold_in(key, 103), kv_shape())


def draw_kv_square(key, part):
    return square_field(jax.random.fold_in(key, 104), kv_shape())


def draw_exp_param(key, part):
    return param_field(jax.random.fold_in(key, 201), exp_shape())


def draw_exp_grad(key, part):
    return gradient_field(jax.random.fold_in(key, 202), exp_shape(), 2)


def draw_exp_mean(key, part):
    return mean_field(jax.random.fold_in(key, 203), exp_shape())


def draw_exp_square(key, part):
    return square_field(jax.random.fold_in(key, 204), exp_shape())


def draw_expert_owner(key, part):
    empty_key, double_key, order_key = jax.random.split(jax.random.fold_in(key, 301), 3)
    empty_shard = jax.random.randint(empty_key, (), 1, N_EXPERT - 1, dtype=jnp.int32)
    base = jnp.arange(N_EXPERT - 1, dtype=jnp.int32)
    present = jnp.where(base >= empty_shard, base + 1, base).astype(jnp.int32)
    doubled = jax.random.randint(double_key, (1,), 0, N_EXPERT - 1, dtype=jnp.int32)
    pattern = jnp.concatenate([doubled, jnp.arange(EXPERTS - 1, dtype=jnp.int32)])
    owners = jnp.take(present, pattern)
    order = jax.random.permutation(order_key, EXPERTS).astype(jnp.int32)
    return jnp.take(owners, order).astype(jnp.int32)


def setup_inputs(seed: int = 0) -> dict:
    arg_keys = jax.random.split(jax.random.key(seed), 10)
    kv_param = draw_kv_param(jax.random.fold_in(arg_keys[9], 71), 0)
    kv_grad = draw_kv_grad(jax.random.fold_in(arg_keys[9], 71), 0)
    kv_mean = draw_kv_mean(jax.random.fold_in(arg_keys[9], 71), 0)
    kv_square = draw_kv_square(jax.random.fold_in(arg_keys[9], 71), 0)
    exp_param = draw_exp_param(jax.random.fold_in(arg_keys[9], 71), 0)
    exp_grad = draw_exp_grad(jax.random.fold_in(arg_keys[9], 71), 0)
    exp_mean = draw_exp_mean(jax.random.fold_in(arg_keys[9], 71), 0)
    exp_square = draw_exp_square(jax.random.fold_in(arg_keys[9], 71), 0)
    expert_owner = draw_expert_owner(jax.random.fold_in(arg_keys[9], 71), 0)
    return dict(kv_param=kv_param, kv_grad=kv_grad, kv_mean=kv_mean, kv_square=kv_square, exp_param=exp_param, exp_grad=exp_grad, exp_mean=exp_mean, exp_square=exp_square, expert_owner=expert_owner)


beta_one = 0.9
beta_two = 0.95
learn_rate = 0.25
decay_rate = 0.01
adam_eps = 1e-08
step_count = 20.0
clip_norm = 1.0
scale_eps = 1e-06

def clip_factor(grad_total):
    return jnp.minimum(1.0, clip_norm / (jnp.sqrt(grad_total) + 1e-06))

def adam_update(master, gradient, moment_one, moment_two, factor):
    scaled = factor * gradient
    mean_new = beta_one * moment_one + (1.0 - beta_one) * scaled
    square_new = beta_two * moment_two + (1.0 - beta_two) * scaled * scaled
    corr_one = 1.0 - beta_one ** step_count
    corr_two = 1.0 - beta_two ** step_count
    update = mean_new / corr_one / (jnp.sqrt(square_new / corr_two) + adam_eps)
    return master - learn_rate * (update + decay_rate * master)

def quantize(master):
    weights = lax.optimization_barrier(master.astype(jnp.bfloat16)).astype(jnp.float32)
    magnitude = lax.optimization_barrier(jnp.max(jnp.abs(weights), axis=(-2, -1)))
    values = (weights / (magnitude[..., None, None] + scale_eps)).astype(jnp.bfloat16)
    return (values, magnitude)

def slot_table(owner, shard_count):
    count = owner.shape[0]
    positions = jnp.arange(count, dtype=jnp.int32)
    earlier_same = (owner[:, None] == owner[None, :]) & (positions[None, :] < positions[:, None])
    slot_rank = lax.optimization_barrier(jnp.sum(earlier_same.astype(jnp.int32), axis=1))
    shard_ids = jnp.arange(shard_count, dtype=jnp.int32)
    slot_ids = jnp.arange(SLOTS, dtype=jnp.int32)
    matched = (owner[None, None, :] == shard_ids[:, None, None]) & (slot_rank[None, None, :] == slot_ids[None, :, None])
    occupied = jnp.any(matched, axis=2)
    chosen = lax.optimization_barrier(jnp.sum(matched.astype(jnp.int32) * positions[None, None, :], axis=2))
    return (chosen, occupied)

def reference(kv_param, kv_grad, kv_mean, kv_square, exp_param, exp_grad, exp_mean, exp_square, expert_owner):
    grad_total = jnp.sum(kv_grad * kv_grad) + jnp.sum(exp_grad * exp_grad)
    factor = clip_factor(grad_total)
    kv_param_new = adam_update(kv_param, kv_grad, kv_mean, kv_square, factor)
    exp_param_new = adam_update(exp_param, exp_grad, exp_mean, exp_square, factor)
    kv_values, kv_magnitude = quantize(kv_param_new)
    exp_values, exp_magnitude = quantize(exp_param_new)
    chosen, occupied = slot_table(expert_owner, N_EXPERT)
    chosen = chosen.reshape(-1)
    occupied = occupied.reshape(-1)
    picked_values = jnp.take(exp_values, chosen, axis=0)
    picked_scales = jnp.take(exp_magnitude, chosen, axis=0)
    exp_rollout = jnp.where(occupied[:, None, None, None, None], picked_values, jnp.zeros_like(picked_values))
    exp_scales = jnp.where(occupied[:, None, None], picked_scales, jnp.zeros_like(picked_scales))
    return (kv_param_new, exp_param_new, kv_values, kv_magnitude, exp_rollout, exp_scales)
```

```python
import jax
import jax.numpy as jnp
from jax import lax
from jax.experimental import pallas as pl
from jax.experimental.pallas import tpu as pltpu
from jax.sharding import Mesh, PartitionSpec as P

SLOTS = 2
EXPERTS = 4
BLK = 128
LANES = 128

beta_one = 0.9
beta_two = 0.95
learn_rate = 0.25
decay_rate = 0.01
adam_eps = 1e-08
step_count = 20.0
clip_norm = 1.0
scale_eps = 1e-06

REPLICA = ("x", "yl", "c")
SHARD = ("x", "yl", "c", "z")
VMEM = pltpu.VMEM
SMEM = pltpu.SMEM


def ring(n, k):
    return [(i, (i + k) % n) for i in range(n)]


def sum_of_squares(kv_grad, exp_grad):
    def kernel(kv_ref, exp_ref, out_ref):
        total = jnp.zeros((8, LANES), jnp.float32)
        for i in range(2):
            g = kv_ref[i, 0]
            total += jnp.sum((g * g).reshape(BLK // 8, 8, LANES), axis=0)
        for e in range(EXPERTS):
            for j in range(3):
                g = exp_ref[e, 0, j]
                total += jnp.sum((g * g).reshape(BLK // 8, 8, LANES), axis=0)
        out_ref[...] = total

    return pl.pallas_call(
        kernel,
        out_shape=jax.ShapeDtypeStruct((8, LANES), jnp.float32),
        in_specs=[pl.BlockSpec(memory_space=VMEM)] * 2,
        out_specs=pl.BlockSpec(memory_space=VMEM),
        name="sum_of_squares",
    )(kv_grad, exp_grad)


def sum_over_devices(v):
    for axis in ("c", "yl", "yh"):
        v = v + lax.ppermute(v, axis, ring(2, 1))
    for axis in ("x", "z"):
        others = [lax.ppermute(v, axis, ring(4, k)) for k in (1, 2, 3)]
        v = v + others[0] + others[1] + others[2]
    return v


def adam(master, gradient, moment_one, moment_two, factor):
    scaled = factor * gradient
    mean_new = beta_one * moment_one + (1.0 - beta_one) * scaled
    square_new = beta_two * moment_two + (1.0 - beta_two) * scaled * scaled
    corr_one = 1.0 - beta_one**step_count
    corr_two = 1.0 - beta_two**step_count
    update = mean_new / corr_one / (jnp.sqrt(square_new / corr_two) + adam_eps)
    return master - learn_rate * (update + decay_rate * master)


def slot_of(owner, shard, slot):
    chosen = jnp.int32(0)
    occupied = jnp.int32(0)
    for e in range(EXPERTS):
        rank = jnp.int32(0)
        for f in range(e):
            rank += (owner[f] == owner[e]).astype(jnp.int32)
        matched = jnp.logical_and(owner[e] == shard, rank == slot).astype(jnp.int32)
        chosen += matched * e
        occupied += matched
    return chosen, occupied


def update(place, owner, total, kv, exp):
    def kernel(place_ref, owner_ref, total_ref, *refs):
        kv_in, exp_in = refs[0:4], refs[4:8]
        kv_new, exp_new, kv_val, routed, scales, values = refs[8:]
        norm = jnp.sqrt(jnp.sum(total_ref[...], keepdims=True)) + 1e-06
        factor = jnp.minimum(1.0, clip_norm / norm)
        lane = lax.broadcasted_iota(jnp.int32, (1, LANES), 1)
        mine = lane == place_ref[0]
        scales[...] = jnp.zeros_like(scales)

        def block(ins, out, val, at, to, row):
            new = adam(ins[0][at], ins[1][at], ins[2][at], ins[3][at], factor)
            out[at] = new
            weights = new.astype(jnp.bfloat16).astype(jnp.float32)
            magnitude = jnp.max(jnp.abs(weights), keepdims=True)
            val[to] = (weights / (magnitude + scale_eps)).astype(jnp.bfloat16)
            scales[pl.ds(row, 1), :] = jnp.where(mine, magnitude, 0.0)

        for i in range(2):
            block(kv_in, kv_new, kv_val, (i, 0), (i, 0), i)
        for e in range(EXPERTS):
            for j in range(3):
                block(exp_in, exp_new, values, (e, 0, j), (e, j), 2 + 3 * e + j)
        owners = [owner_ref[e] for e in range(EXPERTS)]
        for z in range(4):
            for s in range(SLOTS):
                chosen, occupied = slot_of(owners, z, s)
                picked = values[chosen]
                routed[z, s] = jnp.where(occupied > 0, picked, jnp.zeros_like(picked))

    f32, bf16 = jnp.float32, jnp.bfloat16
    return pl.pallas_call(
        kernel,
        out_shape=(
            jax.ShapeDtypeStruct((2, 1, BLK, BLK), f32),
            jax.ShapeDtypeStruct((EXPERTS, 1, 3, BLK, BLK), f32),
            jax.ShapeDtypeStruct((2, 1, BLK, BLK), bf16),
            jax.ShapeDtypeStruct((4, SLOTS, 3, BLK, BLK), bf16),
            jax.ShapeDtypeStruct((16, LANES), f32),
        ),
        in_specs=[pl.BlockSpec(memory_space=SMEM)] * 2 + [pl.BlockSpec(memory_space=VMEM)] * 9,
        out_specs=[pl.BlockSpec(memory_space=VMEM)] * 5,
        scratch_shapes=[pltpu.VMEM((EXPERTS, 3, BLK, BLK), bf16)],
        compiler_params=pltpu.CompilerParams(vmem_limit_bytes=32 * 1024 * 1024),
        name="update",
    )(place, owner, total, *kv, *exp)


def per_device(
    kv_param, kv_grad, kv_mean, kv_square, exp_param, exp_grad, exp_mean, exp_square, expert_owner
):
    total = sum_over_devices(sum_of_squares(kv_grad, exp_grad))
    place = lax.axis_index(SHARD).astype(jnp.int32).reshape(1)
    kv_new, exp_new, kv_val, routed, scales = update(
        place,
        expert_owner,
        total,
        (kv_param, kv_grad, kv_mean, kv_square),
        (exp_param, exp_grad, exp_mean, exp_square),
    )
    arrived = lax.all_to_all(routed, "z", 0, 0, tiled=True)
    arrived = arrived.transpose(1, 0, 2, 3, 4).reshape(SLOTS, 1, 12, BLK, BLK)
    exp_rollout = lax.all_gather(arrived, REPLICA, axis=2, tiled=True)
    kv_plane = lax.all_gather(kv_val, "z", axis=1, tiled=True)
    kv_rollout = lax.all_gather(kv_plane, REPLICA, axis=1, tiled=True)
    for axis in ("c", "x", "yl", "z"):
        scales = lax.psum(scales, axis)
    kv_scales = scales[0:2, 0:64]
    by_expert = scales[2:14, 0:64].reshape(EXPERTS, 3, 64).transpose(0, 2, 1).reshape(EXPERTS, 192)
    shard = lax.axis_index("z").astype(jnp.int32)
    rows = []
    for s in range(SLOTS):
        chosen, occupied = slot_of(expert_owner, shard, s)
        row = lax.dynamic_index_in_dim(by_expert, chosen, 0, keepdims=False)
        rows.append(jnp.where(occupied > 0, row, 0.0))
    exp_scales = jnp.stack(rows).reshape(SLOTS, 1, 192)
    return kv_new, exp_new, kv_rollout, kv_scales, exp_rollout, exp_scales


def solution(mesh):
    fine = Mesh(mesh.devices.reshape(4, 2, 2, 4, 2), ("x", "yl", "c", "z", "yh"))
    kv = P("yh", SHARD, None, None)
    exp = P(None, "yh", SHARD, None, None)
    return jax.shard_map(
        per_device,
        mesh=fine,
        in_specs=(kv, kv, kv, kv, exp, exp, exp, exp, P()),
        out_specs=(
            kv,
            exp,
            P("yh", None, None, None),
            P("yh", None),
            P("z", "yh", None, None, None),
            P("z", "yh", None),
        ),
        check_vma=False,
    )
```

```python
import jax
import jax.numpy as jnp
from jax import lax
from jax.experimental import pallas as pl
from jax.experimental.pallas import tpu as pltpu
from jax.sharding import Mesh, PartitionSpec as P

SLOTS = 2
EXPERTS = 4
BLK = 128
LANES = 128

beta_one = 0.9
beta_two = 0.95
learn_rate = 0.25
decay_rate = 0.01
adam_eps = 1e-08
step_count = 20.0
clip_norm = 1.0
scale_eps = 1e-06

REPLICA = ("x", "yl", "c")
SHARD = ("x", "yl", "c", "z")
VMEM = pltpu.VMEM
SMEM = pltpu.SMEM

TILE = 16
EXP_T, KV_T = 24, 8
PART_T = EXP_T + KV_T + 1
FULL_T = 4 * (EXP_T + KV_T) + 1


def ring(n, k):
    return [(i, (i + k) % n) for i in range(n)]


def sum_of_squares(kv_grad, exp_grad):
    def kernel(kv_ref, exp_ref, out_ref):
        total = jnp.zeros((8, LANES), jnp.float32)
        for i in range(2):
            g = kv_ref[i, 0]
            total += jnp.sum((g * g).reshape(BLK // 8, 8, LANES), axis=0)
        for e in range(EXPERTS):
            for j in range(3):
                g = exp_ref[e, 0, j]
                total += jnp.sum((g * g).reshape(BLK // 8, 8, LANES), axis=0)
        out_ref[...] = total

    return pl.pallas_call(
        kernel,
        out_shape=jax.ShapeDtypeStruct((8, LANES), jnp.float32),
        in_specs=[pl.BlockSpec(memory_space=VMEM)] * 2,
        out_specs=pl.BlockSpec(memory_space=VMEM),
        name="sum_of_squares",
    )(kv_grad, exp_grad)


def sum_over_devices(v):
    for axis in ("c", "yl", "yh"):
        v = v + lax.ppermute(v, axis, ring(2, 1))
    for axis in ("x", "z"):
        others = [lax.ppermute(v, axis, ring(4, k)) for k in (1, 2, 3)]
        v = v + others[0] + others[1] + others[2]
    return v


def adam(master, gradient, moment_one, moment_two, factor):
    scaled = factor * gradient
    mean_new = beta_one * moment_one + (1.0 - beta_one) * scaled
    square_new = beta_two * moment_two + (1.0 - beta_two) * scaled * scaled
    corr_one = 1.0 - beta_one**step_count
    corr_two = 1.0 - beta_two**step_count
    update = mean_new / corr_one / (jnp.sqrt(square_new / corr_two) + adam_eps)
    return master - learn_rate * (update + decay_rate * master)


def slot_of(owner, shard, slot):
    chosen = jnp.int32(0)
    occupied = jnp.int32(0)
    for e in range(EXPERTS):
        rank = jnp.int32(0)
        for f in range(e):
            rank += (owner[f] == owner[e]).astype(jnp.int32)
        matched = jnp.logical_and(owner[e] == shard, rank == slot).astype(jnp.int32)
        chosen += matched * e
        occupied += matched
    return chosen, occupied


def update(place, owner, total, kv, exp):
    def kernel(place_ref, owner_ref, total_ref, *refs):
        kv_hbm, exp_hbm = refs[0:4], refs[4:8]
        kv_new, exp_new = refs[8:10]
        parts = refs[10:14]
        kv_in, exp_in, kv_val, values, sems = refs[14:]
        kv_copies = [
            pltpu.make_async_copy(kv_hbm[a], kv_in.at[a], sems.at[EXPERTS, a]) for a in range(4)
        ]
        exp_copies = [
            [
                pltpu.make_async_copy(exp_hbm[a].at[e, 0], exp_in.at[a, e], sems.at[e, a])
                for a in range(4)
            ]
            for e in range(EXPERTS)
        ]
        for copies in [kv_copies] + exp_copies:
            for copy in copies:
                copy.start()
        norm = jnp.sqrt(jnp.sum(total_ref[...], keepdims=True)) + 1e-06
        factor = jnp.minimum(1.0, clip_norm / norm)
        row = lax.broadcasted_iota(jnp.int32, (TILE, LANES), 0)
        flat = row * LANES + lax.broadcasted_iota(jnp.int32, (TILE, LANES), 1)

        def block(ins, at):
            new = adam(ins[0, *at], ins[1, *at], ins[2, *at], ins[3, *at], factor)
            weights = new.astype(jnp.bfloat16).astype(jnp.float32)
            magnitude = jnp.max(jnp.abs(weights), keepdims=True)
            scaled = weights / (magnitude + scale_eps)
            return new, scaled.reshape(BLK // TILE, TILE, LANES).astype(jnp.bfloat16), magnitude

        for copy in kv_copies:
            copy.wait()
        kv_mag = []
        for i in range(2):
            new, val, magnitude = block(kv_in, (i, 0))
            kv_new[i, 0] = new
            kv_val[i] = val
            kv_mag.append(magnitude)
        exp_mag = []
        for e in range(EXPERTS):
            for copy in exp_copies[e]:
                copy.wait()
            for j in range(3):
                new, val, magnitude = block(exp_in, (e, j))
                exp_new[e, 0, j] = new
                values[e, 8 * j : 8 * j + 8] = val
                exp_mag.append(magnitude)
        place = place_ref[0]
        shard = lax.rem(place, 4)
        owners = [owner_ref[e] for e in range(EXPERTS)]
        for k in range(4):
            for h in range(SLOTS):
                chosen, occupied = slot_of(owners, lax.rem(shard + k, 4), h)
                picked = values[chosen]
                parts[k][h, 0:EXP_T] = jnp.where(occupied > 0, picked, jnp.zeros_like(picked))
                parts[k][h, EXP_T : EXP_T + KV_T] = kv_val[h]
                tile = jnp.where(flat == 2 * LANES + place, kv_mag[h], 0.0)
                for j in range(3):
                    magnitude = jnp.zeros((1, 1), jnp.float32)
                    for e in range(EXPERTS):
                        held = jnp.logical_and(chosen == e, occupied > 0)
                        magnitude = jnp.where(held, exp_mag[3 * e + j], magnitude)
                    tile = jnp.where(flat == place * 3 + j, magnitude, tile)
                parts[k][h, EXP_T + KV_T] = tile.astype(jnp.bfloat16)

    f32, bf16 = jnp.float32, jnp.bfloat16
    return pl.pallas_call(
        kernel,
        out_shape=(
            jax.ShapeDtypeStruct((2, 1, BLK, BLK), f32),
            jax.ShapeDtypeStruct((EXPERTS, 1, 3, BLK, BLK), f32),
        )
        + (jax.ShapeDtypeStruct((SLOTS, PART_T, TILE, LANES), bf16),) * 4,
        in_specs=[pl.BlockSpec(memory_space=SMEM)] * 2
        + [pl.BlockSpec(memory_space=VMEM)]
        + [pl.BlockSpec(memory_space=pl.ANY)] * 8,
        out_specs=[pl.BlockSpec(memory_space=VMEM)] * 6,
        scratch_shapes=[
            pltpu.VMEM((4, 2, 1, BLK, BLK), f32),
            pltpu.VMEM((4, EXPERTS, 3, BLK, BLK), f32),
            pltpu.VMEM((2, KV_T, TILE, LANES), bf16),
            pltpu.VMEM((EXPERTS, EXP_T, TILE, LANES), bf16),
            pltpu.SemaphoreType.DMA((EXPERTS + 1, 4)),
        ],
        compiler_params=pltpu.CompilerParams(vmem_limit_bytes=48 * 1024 * 1024),
        name="update",
    )(place, owner, total, *kv, *exp)


def join(place, parts):
    def kernel(place_ref, *refs):
        out = refs[4]
        shard = lax.rem(place_ref[0], 4)
        for h in range(SLOTS):
            tile = jnp.zeros((TILE, LANES), jnp.float32)
            for k in range(4):
                z = lax.rem(shard - k + 4, 4)
                out[h, pl.ds(z * EXP_T, EXP_T)] = refs[k][h, 0:EXP_T]
                out[h, pl.ds(4 * EXP_T + z * KV_T, KV_T)] = refs[k][h, EXP_T : EXP_T + KV_T]
                tile += refs[k][h, EXP_T + KV_T].astype(jnp.float32)
            out[h, FULL_T - 1] = tile.astype(jnp.bfloat16)

    return pl.pallas_call(
        kernel,
        out_shape=jax.ShapeDtypeStruct((SLOTS, FULL_T, TILE, LANES), jnp.bfloat16),
        in_specs=[pl.BlockSpec(memory_space=SMEM)] + [pl.BlockSpec(memory_space=VMEM)] * 4,
        out_specs=pl.BlockSpec(memory_space=VMEM),
        compiler_params=pltpu.CompilerParams(vmem_limit_bytes=16 * 1024 * 1024),
        name="join",
    )(place, *parts)


def source(place, steps, over_y, over_c):
    replica = lax.div(place, 4)
    x, y, c = lax.div(replica, 4), lax.rem(lax.div(replica, 2), 2), lax.rem(replica, 2)
    c = 1 - c if over_c else c
    y = 1 - y if over_y else y
    x = lax.rem(x + 4 + jnp.where(c == 0, -steps, steps), 4)
    return x * 4 + y * 2 + c


EXP_OUT = jax.ShapeDtypeStruct((SLOTS, 16 * 4 * EXP_T, TILE, LANES), jnp.bfloat16)
KV_OUT = jax.ShapeDtypeStruct((SLOTS, 16 * 4 * KV_T, TILE, LANES), jnp.bfloat16)


def lay(place, pieces, outs=None, tiles=None):
    arrays = [p[0] for p in pieces]
    more = [p[0] for p in tiles] if tiles else []
    count = sum(2 if p[1] is None else 1 for p in pieces)

    def views(p, ref):
        if p[1] is None:
            return [(h, ref.at[h]) for h in range(SLOTS)]
        return [(p[1], ref)]

    every = (pieces + tiles) if tiles else []
    seen = sum(2 if p[1] is None else 1 for p in every)

    def kernel(place_ref, *refs):
        n, m, o = len(arrays), len(more), 2 if outs else 0
        ins, late = refs[:n], refs[n : n + m]
        rest = refs[n + m + o :]
        exp_out, kv_out = rest[0], rest[1]
        sems = rest[-1]
        here = place_ref[0]
        copies = []
        gets = []
        if tiles:
            exp_scales, kv_scales, held, tile_sems = rest[2], rest[3], rest[4], rest[5]
            i = 0
            slots = []
            for p, ref in zip(every, ins + late):
                for h, view in views(p, ref):
                    gets.append(pltpu.make_async_copy(view.at[FULL_T - 1], held.at[i], tile_sems.at[i]))
                    slots.append(h)
                    i += 1
        i = 0
        for p, ref in zip(pieces, ins):
            at = source(here, *p[2:])
            for h, view in views(p, ref):
                n_exp, n_kv = 4 * EXP_T, 4 * KV_T
                copies.append(
                    pltpu.make_async_copy(
                        view.at[pl.ds(0, n_exp)],
                        exp_out.at[h, pl.ds(at * n_exp, n_exp)],
                        sems.at[i, 0],
                    )
                )
                copies.append(
                    pltpu.make_async_copy(
                        view.at[pl.ds(n_exp, n_kv)],
                        kv_out.at[h, pl.ds(at * n_kv, n_kv)],
                        sems.at[i, 1],
                    )
                )
                i += 1
        for copy in gets + copies:
            copy.start()
        if tiles:
            for get in gets:
                get.wait()
            for h in range(SLOTS):
                total = jnp.zeros((TILE, LANES), jnp.float32)
                for i, slot in enumerate(slots):
                    if slot == h:
                        total += held[i].astype(jnp.float32)
                exp_scales[h, 0:1, :] = total[0:1, :]
                exp_scales[h, 1:2, :] = total[1:2, :]
                kv_scales[h : h + 1, :] = total[2:3, :]
        for copy in copies:
            copy.wait()

    out_shape = [EXP_OUT, KV_OUT]
    out_specs = [pl.BlockSpec(memory_space=pl.ANY)] * 2
    scratch = []
    if tiles:
        out_shape += [
            jax.ShapeDtypeStruct((SLOTS, 2, LANES), jnp.float32),
            jax.ShapeDtypeStruct((SLOTS, LANES), jnp.float32),
        ]
        out_specs += [pl.BlockSpec(memory_space=VMEM)] * 2
        scratch += [
            pltpu.VMEM((seen, TILE, LANES), jnp.bfloat16),
            pltpu.SemaphoreType.DMA((seen,)),
        ]
    scratch.append(pltpu.SemaphoreType.DMA((count, 2)))
    operands = arrays + more + (list(outs) if outs else [])
    first = 1 + len(arrays) + len(more)
    return pl.pallas_call(
        kernel,
        out_shape=tuple(out_shape),
        in_specs=[pl.BlockSpec(memory_space=SMEM)]
        + [pl.BlockSpec(memory_space=pl.ANY)] * len(operands),
        out_specs=tuple(out_specs),
        scratch_shapes=scratch,
        input_output_aliases={first: 0, first + 1: 1} if outs else {},
        compiler_params=pltpu.CompilerParams(vmem_limit_bytes=4 * 1024 * 1024),
        cost_estimate=pl.CostEstimate(flops=0, transcendentals=0, bytes_accessed=count * 2**20),
        name="lay",
    )(place, *operands)


def swap_core(v):
    return lax.ppermute(v, "c", ring(2, 1))


def swap_y(v):
    return lax.ppermute(v, "yl", ring(2, 1))


def along_x(v):
    pairs = [(2 * x + c, 2 * ((x + (3 if c else 1)) % 4) + c) for x in range(4) for c in range(2)]
    return lax.ppermute(v, ("x", "c"), pairs)


def per_device(
    kv_param, kv_grad, kv_mean, kv_square, exp_param, exp_grad, exp_mean, exp_square, expert_owner
):
    total = sum_over_devices(sum_of_squares(kv_grad, exp_grad))
    place = lax.axis_index(SHARD).astype(jnp.int32).reshape(1)
    kv_new, exp_new, *parts = update(
        place,
        expert_owner,
        total,
        (kv_param, kv_grad, kv_mean, kv_square),
        (exp_param, exp_grad, exp_mean, exp_square),
    )
    parts = [parts[0]] + [lax.ppermute(parts[k], "z", ring(4, k)) for k in (1, 2, 3)]
    p0 = join(place, parts)
    q0 = swap_y(p0)
    p1 = along_x(p0)
    p2 = along_x(p1)
    p3 = along_x(p2)
    a1 = along_x(q0[0])
    a2 = along_x(a1)
    a3 = along_x(a2)
    b1, b2, b3 = swap_y(p1[1]), swap_y(p2[1]), swap_y(p3[1])
    own = [
        (p0, None, 0, False),
        (p1, None, 1, False),
        (p2, None, 2, False),
        (q0, None, 0, True),
        (p3, None, 3, False),
        (b1, 1, 1, True),
        (a1, 0, 1, True),
        (b2, 1, 2, True),
        (a2, 0, 2, True),
        (b3, 1, 3, True),
        (a3, 0, 3, True),
    ]
    pieces = []
    for p in own:
        pieces.append((*p, False))
        pieces.append((swap_core(p[0]), *p[1:], True))
    outs = lay(place, pieces[:8])
    outs = lay(place, pieces[8:16], outs)
    exp_rollout, kv_rollout, exp_scales, kv_scales = lay(place, pieces[16:], outs, pieces[:16])
    return (
        kv_new,
        exp_new,
        kv_rollout.reshape(2, 64, BLK, BLK),
        kv_scales[:, 0:64],
        exp_rollout.reshape(SLOTS, 1, 192, BLK, BLK),
        exp_scales.reshape(SLOTS, 1, 2 * LANES)[:, :, 0:192],
    )


def solution(mesh):
    fine = Mesh(mesh.devices.reshape(4, 2, 2, 4, 2), ("x", "yl", "c", "z", "yh"))
    kv = P("yh", SHARD, None, None)
    exp = P(None, "yh", SHARD, None, None)
    return jax.shard_map(
        per_device,
        mesh=fine,
        in_specs=(kv, kv, kv, kv, exp, exp, exp, exp, P()),
        out_specs=(
            kv,
            exp,
            P("yh", None, None, None),
            P("yh", None),
            P("z", "yh", None, None, None),
            P("z", "yh", None),
        ),
        check_vma=False,
    )
```

```python
import jax
import jax.numpy as jnp
from jax import lax
from jax.experimental import pallas as pl
from jax.experimental.pallas import tpu as pltpu
from jax.sharding import Mesh, PartitionSpec as P

SLOTS = 2
EXPERTS = 4
BLK = 128
LANES = 128

beta_one = 0.9
beta_two = 0.95
learn_rate = 0.25
decay_rate = 0.01
adam_eps = 1e-08
step_count = 20.0
clip_norm = 1.0
scale_eps = 1e-06

REPLICA = ("x", "yl", "c")
SHARD = ("x", "yl", "c", "z")
VMEM = pltpu.VMEM
SMEM = pltpu.SMEM

TILE = 16
SLOT_T = 24
PART_T = 1 + 2 * SLOT_T
FULL_T = 1 + 8 * SLOT_T
A_T = 129
KV_T = 8
PLANE_T = 2 * 8 * KV_T + 1


def ring(n, k):
    return [(i, (i + k) % n) for i in range(n)]


def sum_of_squares(kv_grad, exp_grad):
    def kernel(kv_ref, exp_ref, out_ref):
        total = jnp.zeros((8, LANES), jnp.float32)
        for i in range(2):
            g = kv_ref[i, 0]
            total += jnp.sum((g * g).reshape(BLK // 8, 8, LANES), axis=0)
        for e in range(EXPERTS):
            for j in range(3):
                g = exp_ref[e, 0, j]
                total += jnp.sum((g * g).reshape(BLK // 8, 8, LANES), axis=0)
        out_ref[...] = total

    return pl.pallas_call(
        kernel,
        out_shape=jax.ShapeDtypeStruct((8, LANES), jnp.float32),
        in_specs=[pl.BlockSpec(memory_space=VMEM)] * 2,
        out_specs=pl.BlockSpec(memory_space=VMEM),
        name="sum_of_squares",
    )(kv_grad, exp_grad)


def sum_over_devices(v):
    for axis in ("x", "z"):
        others = [lax.ppermute(v, axis, ring(4, k)) for k in (1, 2, 3)]
        v = v + others[0] + others[1] + others[2]
    for axis in ("yl", "yh", "c"):
        v = v + lax.ppermute(v, axis, ring(2, 1))
    return v


def adam(master, gradient, moment_one, moment_two, factor):
    scaled = factor * gradient
    mean_new = beta_one * moment_one + (1.0 - beta_one) * scaled
    square_new = beta_two * moment_two + (1.0 - beta_two) * scaled * scaled
    corr_one = 1.0 - beta_one**step_count
    corr_two = 1.0 - beta_two**step_count
    update = mean_new / corr_one / (jnp.sqrt(square_new / corr_two) + adam_eps)
    return master - learn_rate * (update + decay_rate * master)


def slot_of(owner, shard, slot):
    chosen = jnp.int32(0)
    occupied = jnp.int32(0)
    for e in range(EXPERTS):
        rank = jnp.int32(0)
        for f in range(e):
            rank += (owner[f] == owner[e]).astype(jnp.int32)
        matched = jnp.logical_and(owner[e] == shard, rank == slot).astype(jnp.int32)
        chosen += matched * e
        occupied += matched
    return chosen, occupied


def update(place, owner, total, kv, exp):
    def kernel(place_ref, owner_ref, total_ref, *refs):
        kv_hbm, exp_hbm = refs[0:4], refs[4:8]
        kv_new, exp_new = refs[8:10]
        parts, kv_part = refs[10:14], refs[14]
        kv_in, exp_in, values, tiles, sems = refs[15:]
        kv_copies = [
            pltpu.make_async_copy(kv_hbm[a], kv_in.at[a], sems.at[EXPERTS, a]) for a in range(4)
        ]
        exp_copies = [
            [
                pltpu.make_async_copy(exp_hbm[a].at[e, 0], exp_in.at[a, e], sems.at[e, a])
                for a in range(4)
            ]
            for e in range(EXPERTS)
        ]
        for copies in [kv_copies] + exp_copies:
            for copy in copies:
                copy.start()
        norm = jnp.sqrt(jnp.sum(total_ref[...], keepdims=True)) + 1e-06
        factor = jnp.minimum(1.0, clip_norm / norm)
        row = lax.broadcasted_iota(jnp.int32, (TILE, LANES), 0)
        flat = row * LANES + lax.broadcasted_iota(jnp.int32, (TILE, LANES), 1)

        def block(ins, at):
            new = adam(ins[0, *at], ins[1, *at], ins[2, *at], ins[3, *at], factor)
            weights = new.astype(jnp.bfloat16).astype(jnp.float32)
            magnitude = jnp.max(jnp.abs(weights), keepdims=True)
            scaled = weights / (magnitude + scale_eps)
            return new, scaled.reshape(BLK // TILE, TILE, LANES).astype(jnp.bfloat16), magnitude

        for copy in kv_copies:
            copy.wait()
        place = place_ref[0]
        shard = lax.rem(place, 4)
        kv_tile = jnp.zeros((TILE, LANES), jnp.float32)
        for i in range(2):
            new, val, magnitude = block(kv_in, (i, 0))
            kv_new[i, 0] = new
            kv_part[8 * i : 8 * i + 8] = val
            kv_tile = jnp.where(flat == i * LANES + place, magnitude, kv_tile)
        kv_part[16] = kv_tile.astype(jnp.bfloat16)
        for e in range(EXPERTS):
            for copy in exp_copies[e]:
                copy.wait()
            tile = jnp.zeros((TILE, LANES), jnp.float32)
            for j in range(3):
                new, val, magnitude = block(exp_in, (e, j))
                exp_new[e, 0, j] = new
                values[e, 8 * j : 8 * j + 8] = val
                at = place * 3 + j
                here = jnp.logical_or(flat == at, flat == at + 2 * LANES)
                tile = jnp.where(here, magnitude, tile)
            tiles[e] = tile
        owners = [owner_ref[e] for e in range(EXPERTS)]
        for k in range(4):
            scales = jnp.zeros((TILE, LANES), jnp.float32)
            for h in range(SLOTS):
                chosen, occupied = slot_of(owners, lax.rem(shard + k, 4), h)
                picked = values[chosen]
                at = 1 + h * SLOT_T
                parts[k][at : at + SLOT_T] = jnp.where(
                    occupied > 0, picked, jnp.zeros_like(picked)
                )
                held = jnp.logical_and(lax.div(row, 2) == h, occupied > 0)
                scales = jnp.where(held, tiles[chosen], scales)
            parts[k][0] = scales.astype(jnp.bfloat16)

    f32, bf16 = jnp.float32, jnp.bfloat16
    return pl.pallas_call(
        kernel,
        out_shape=(
            jax.ShapeDtypeStruct((2, 1, BLK, BLK), f32),
            jax.ShapeDtypeStruct((EXPERTS, 1, 3, BLK, BLK), f32),
        )
        + (jax.ShapeDtypeStruct((PART_T, TILE, LANES), bf16),) * 4
        + (jax.ShapeDtypeStruct((17, TILE, LANES), bf16),),
        in_specs=[pl.BlockSpec(memory_space=SMEM)] * 2
        + [pl.BlockSpec(memory_space=VMEM)]
        + [pl.BlockSpec(memory_space=pltpu.HBM)] * 8,
        out_specs=[pl.BlockSpec(memory_space=VMEM)] * 7,
        scratch_shapes=[
            pltpu.VMEM((4, 2, 1, BLK, BLK), f32),
            pltpu.VMEM((4, EXPERTS, 3, BLK, BLK), f32),
            pltpu.VMEM((EXPERTS, SLOT_T, TILE, LANES), bf16),
            pltpu.VMEM((EXPERTS, TILE, LANES), f32),
            pltpu.SemaphoreType.DMA((EXPERTS + 1, 4)),
        ],
        compiler_params=pltpu.CompilerParams(vmem_limit_bytes=60 * 1024 * 1024),
        name="update",
    )(place, owner, total, *kv, *exp)


def join(place, parts):
    def kernel(place_ref, *refs):
        out, out_a, out_b = refs[4:]
        shard = lax.rem(place_ref[0], 4)
        tile = jnp.zeros((TILE, LANES), jnp.float32)
        for k in range(4):
            z = lax.rem(shard - k + 4, 4)
            tile += refs[k][0].astype(jnp.float32)
            for h in range(SLOTS):
                got = refs[k][1 + h * SLOT_T : 1 + (h + 1) * SLOT_T]
                out[pl.ds(1 + 4 * h * SLOT_T + z * SLOT_T, SLOT_T)] = got
        out[0] = tile.astype(jnp.bfloat16)
        out_a[...] = out[0:A_T]
        out_b[...] = out[A_T:FULL_T]

    return pl.pallas_call(
        kernel,
        out_shape=tuple(
            jax.ShapeDtypeStruct((n, TILE, LANES), jnp.bfloat16) for n in (FULL_T, A_T, FULL_T - A_T)
        ),
        in_specs=[pl.BlockSpec(memory_space=SMEM)] + [pl.BlockSpec(memory_space=VMEM)] * 4,
        out_specs=[pl.BlockSpec(memory_space=VMEM)] * 3,
        compiler_params=pltpu.CompilerParams(vmem_limit_bytes=16 * 1024 * 1024),
        name="join",
    )(place, *parts)


def join_kv(place, parts):
    def kernel(place_ref, *refs):
        out = refs[5]
        replica = lax.div(place_ref[0], 4)
        y = lax.rem(lax.div(replica, 2), 2)
        views = [(refs[0], 0, y), (refs[1], 0, 1 - y)]
        for k in (1, 2, 3):
            views += [(refs[k + 1].at[0], k, y), (refs[k + 1].at[1], k, 1 - y)]
        tile = jnp.zeros((TILE, LANES), jnp.float32)
        for ref, steps, at_y in views:
            chip = chip_along(replica, steps) * 2 + at_y
            for h in range(2):
                out[pl.ds(KV_T * (8 * h + chip), KV_T)] = ref[KV_T * h : KV_T * (h + 1)]
            tile += ref[16].astype(jnp.float32)
        out[PLANE_T - 1] = tile.astype(jnp.bfloat16)

    return pl.pallas_call(
        kernel,
        out_shape=jax.ShapeDtypeStruct((PLANE_T, TILE, LANES), jnp.bfloat16),
        in_specs=[pl.BlockSpec(memory_space=SMEM)] + [pl.BlockSpec(memory_space=VMEM)] * 5,
        out_specs=pl.BlockSpec(memory_space=VMEM),
        compiler_params=pltpu.CompilerParams(vmem_limit_bytes=16 * 1024 * 1024),
        name="join_kv",
    )(place, *parts)


def chip_along(replica, steps):
    x, c = lax.div(replica, 4), lax.rem(replica, 2)
    return lax.rem(x + 4 + jnp.where(c == 0, -steps, steps), 4)


EXP_OUT = jax.ShapeDtypeStruct((SLOTS, 16 * 4 * SLOT_T, TILE, LANES), jnp.bfloat16)
KV_OUT = jax.ShapeDtypeStruct((2, 8, 2, 4, KV_T, TILE, LANES), jnp.bfloat16)


SIZE = {"P": FULL_T, "A": A_T, "B": FULL_T - A_T, "K": PLANE_T}
SCALES = {"P": 0, "A": 0, "K": PLANE_T - 1}


def lay(place, own, got, outs=None, pack=False, last=False):
    views = [(n, 0, piece, False) for n, (_, piece) in enumerate(own)]
    for n, (_, held) in enumerate(got):
        at = 0
        for piece in held:
            views.append((len(own) + n, at, piece, True))
            at += SIZE[piece[0]]
    arrays = [array for array, _ in own + got]
    total = sum(SIZE[piece[0]] for _, piece in own)
    with_scales = [view for view in views if view[2][0] != "B"]
    count = 2 * len(views) + (len(own) if pack else 0)

    def kernel(place_ref, *refs):
        ins = refs[: len(arrays)]
        sum_in = refs[len(arrays) + 2] if outs else None
        rest = refs[len(arrays) + (3 if outs else 0) :]
        exp_out, kv_out, results = rest[0], rest[1], rest[2:-3]
        tiles, tile_sems, sems = rest[-3:]
        here = place_ref[0]
        replica, shard = lax.div(here, 4), lax.rem(here, 4)
        copies, gets = [], []

        def copy(src, dst):
            copies.append(pltpu.make_async_copy(src, dst, sems.at[len(copies)]))
            copies[-1].start()

        for i, (n, at, piece, _) in enumerate(with_scales):
            src = ins[n].at[at + SCALES[piece[0]]]
            gets.append(pltpu.make_async_copy(src, tiles.at[i], tile_sems.at[i]))
            gets[-1].start()
        if pack:
            at = 0
            for n, (_, piece) in enumerate(own):
                copy(ins[n], results[1].at[pl.ds(at, SIZE[piece[0]])])
                at += SIZE[piece[0]]
        for n, base, (kind, steps, over_y), over_c in views:
            ref = ins[n]
            c = lax.rem(replica, 2)
            if over_c:
                c = 1 - c
            forward = jnp.where(c == 0, -steps, steps)
            if kind == "K":
                z = lax.rem(shard + 4 + forward, 4)
                for h in range(2):
                    blocks = ref.at[pl.ds(base + 8 * KV_T * h, 8 * KV_T)]
                    copy(blocks.reshape(8, KV_T, TILE, LANES), kv_out.at[h, :, c, z])
                continue
            y = lax.rem(lax.div(replica, 2), 2)
            if over_y:
                y = 1 - y
            x = lax.rem(lax.div(replica, 4) + 4 + forward, 4)
            n = 4 * SLOT_T
            to = (x * 4 + y * 2 + c) * n
            first = A_T - 1 - n
            if kind in "PA":
                copy(ref.at[pl.ds(base + 1, n)], exp_out.at[0, pl.ds(to, n)])
            if kind == "P":
                copy(ref.at[pl.ds(base + 1 + n, n)], exp_out.at[1, pl.ds(to, n)])
            if kind == "A":
                copy(ref.at[pl.ds(base + 1 + n, first)], exp_out.at[1, pl.ds(to, first)])
            if kind == "B":
                copy(ref.at[pl.ds(base, n - first)], exp_out.at[1, pl.ds(to + first, n - first)])
        for get in gets:
            get.wait()
        sums = [jnp.zeros((TILE, LANES), jnp.float32) for _ in range(2)]
        if outs:
            sums = [sum_in[0], sum_in[1]]
        for i, (_, _, piece, _) in enumerate(with_scales):
            sums[piece[0] == "K"] += tiles[i].astype(jnp.float32)
        if last:
            results[0][0] = sums[0][0:2]
            results[0][1] = sums[0][2:4]
            results[1][...] = sums[1][0:2]
        else:
            results[0][0] = sums[0]
            results[0][1] = sums[1]
        for c in copies:
            c.wait()

    out_shape = [EXP_OUT, KV_OUT]
    out_specs = [pl.BlockSpec(memory_space=pl.ANY)] * 2
    if last:
        out_shape += [
            jax.ShapeDtypeStruct((SLOTS, 2, LANES), jnp.float32),
            jax.ShapeDtypeStruct((2, LANES), jnp.float32),
        ]
        out_specs += [pl.BlockSpec(memory_space=VMEM)] * 2
    else:
        out_shape += [jax.ShapeDtypeStruct((2, TILE, LANES), jnp.float32)]
        out_specs += [pl.BlockSpec(memory_space=VMEM)]
    if pack:
        out_shape += [jax.ShapeDtypeStruct((total, TILE, LANES), jnp.bfloat16)]
        out_specs += [pl.BlockSpec(memory_space=pltpu.HBM)]
    first_out = 1 + len(arrays)
    return pl.pallas_call(
        kernel,
        out_shape=tuple(out_shape),
        in_specs=[pl.BlockSpec(memory_space=SMEM)]
        + [pl.BlockSpec(memory_space=pl.ANY)] * (len(arrays) + (2 if outs else 0))
        + [pl.BlockSpec(memory_space=VMEM)] * (1 if outs else 0),
        out_specs=tuple(out_specs),
        scratch_shapes=[
            pltpu.VMEM((len(with_scales), TILE, LANES), jnp.bfloat16),
            pltpu.SemaphoreType.DMA((len(with_scales),)),
            pltpu.SemaphoreType.DMA((count,)),
        ],
        input_output_aliases={first_out: 0, first_out + 1: 1} if outs else {},
        compiler_params=pltpu.CompilerParams(vmem_limit_bytes=4 * 1024 * 1024),
        cost_estimate=pl.CostEstimate(flops=0, transcendentals=0, bytes_accessed=count * 2**19),
        name="lay",
    )(place, *arrays, *(outs or []))


def after(*values):
    return lax.optimization_barrier(values)


def swap_core(v):
    return lax.ppermute(v, "c", ring(2, 1))


def swap_y(v):
    return lax.ppermute(v, "yl", ring(2, 1))


def along_x(v, k=1):
    step = (k, 4 - k)
    pairs = [(2 * x + c, 2 * ((x + step[c]) % 4) + c) for x in range(4) for c in range(2)]
    return lax.ppermute(v, ("x", "c"), pairs)


def along_z(v):
    pairs = [(4 * c + z, 4 * c + (z + (3 if c else 1)) % 4) for c in range(2) for z in range(4)]
    return lax.ppermute(v, ("c", "z"), pairs)


def per_device(
    kv_param, kv_grad, kv_mean, kv_square, exp_param, exp_grad, exp_mean, exp_square, expert_owner
):
    total = sum_over_devices(sum_of_squares(kv_grad, exp_grad))
    place = lax.axis_index(SHARD).astype(jnp.int32).reshape(1)
    kv_new, exp_new, *parts, kv_part = update(
        place,
        expert_owner,
        total,
        (kv_param, kv_grad, kv_mean, kv_square),
        (exp_param, exp_grad, exp_mean, exp_square),
    )
    parts = [parts[0]] + [lax.ppermute(parts[k], "z", ring(4, k)) for k in (1, 2, 3)]
    kv_across = swap_y(kv_part)
    *parts, kv_part, kv_across = after(*parts, kv_part, kv_across)

    p0, a_own, b_own = join(place, parts)
    p1, qa = along_x(p0), swap_y(a_own)
    kv_two = jnp.stack([kv_part, kv_across])
    k1, k2, k3 = (along_x(kv_two, k) for k in (1, 2, 3))
    p1, qa, b_own, k1, k2, k3 = after(p1, qa, b_own, k1, k2, k3)

    w0 = join_kv(place, (kv_part, kv_across, k1, k2, k3))
    p2, a1, qb, b1, w1 = along_x(p1), along_x(qa), swap_y(b_own), swap_y(p1[A_T:FULL_T]), along_z(w0)
    held1 = [("P", 0, False), ("P", 1, False), ("A", 0, True)]
    *outs, pack1 = lay(place, list(zip([p0, p1, qa], held1)), [], pack=True)
    p2, a1, qb, b1, w1, pack1, *outs = after(p2, a1, qb, b1, w1, pack1, *outs)

    p3, a2, b2, w2 = along_x(p2), along_x(a1), swap_y(p2[A_T:FULL_T]), along_z(w1)
    got1 = swap_core(pack1)
    held2 = [("P", 2, False), ("A", 1, True), ("B", 0, True), ("B", 1, True)]
    held2 += [("K", 0, False), ("K", 1, False)]
    own = [p2, a1, qb, b1, w0, w1]
    *outs, pack2 = lay(place, list(zip(own, held2)), [], outs, pack=True)
    p3, a2, b2, w2, got1, pack2, *outs = after(p3, a2, b2, w2, got1, pack2, *outs)

    a3, b3, w3 = along_x(a2), swap_y(p3[A_T:FULL_T]), along_z(w2)
    got2, got3 = swap_core(pack2), swap_core(p3)
    held3 = [("A", 2, True), ("B", 2, True), ("K", 2, False)]
    own = list(zip([a2, b2, w2], held3))
    *outs, pack3 = lay(place, own, [(got1, held1)], outs, pack=True)
    a3, b3, w3, got2, got3, pack3, *outs = after(a3, b3, w3, got2, got3, pack3, *outs)

    held4 = [("A", 3, True), ("B", 3, True), ("K", 3, False)]
    got4 = [(swap_core(v), [p]) for v, p in zip((a3, b3, w3), held4)]
    got4.append((swap_core(pack3), held3))
    own = list(zip([p3, a3, b3, w3], [("P", 3, False)] + held4))
    outs = lay(place, own, [(got2, held2), (got3, [("P", 3, False)])], outs)
    exp_rollout, kv_rollout, exp_scales, kv_scales = lay(place, [], got4, outs, last=True)
    return (
        kv_new,
        exp_new,
        kv_rollout.reshape(2, 64, BLK, BLK),
        kv_scales[:, 0:64],
        exp_rollout.reshape(SLOTS, 1, 192, BLK, BLK),
        exp_scales.reshape(SLOTS, 1, 2 * LANES)[:, :, 0:192],
    )


def solution(mesh):
    fine = Mesh(mesh.devices.reshape(4, 2, 2, 4, 2), ("x", "yl", "c", "z", "yh"))
    kv = P("yh", SHARD, None, None)
    exp = P(None, "yh", SHARD, None, None)
    return jax.shard_map(
        per_device,
        mesh=fine,
        in_specs=(kv, kv, kv, kv, exp, exp, exp, exp, P()),
        out_specs=(
            kv,
            exp,
            P("yh", None, None, None),
            P("yh", None),
            P("z", "yh", None, None, None),
            P("z", "yh", None),
        ),
        check_vma=False,
    )
```

```python
import jax
import jax.numpy as jnp
from jax import lax
from jax.experimental import pallas as pl
from jax.experimental.pallas import tpu as pltpu
from jax.sharding import Mesh, PartitionSpec as P

SLOTS = 2
EXPERTS = 4
BLK = 128
LANES = 128

beta_one = 0.9
beta_two = 0.95
learn_rate = 0.25
decay_rate = 0.01
adam_eps = 1e-08
step_count = 20.0
clip_norm = 1.0
scale_eps = 1e-06

REPLICA = ("x", "yl", "c")
SHARD = ("x", "yl", "c", "z")
VMEM = pltpu.VMEM
SMEM = pltpu.SMEM

TILE = 16
SLOT_T = 24
PART_T = 1 + 2 * SLOT_T
FULL_T = 1 + 8 * SLOT_T
A_T = 129
KV_T = 8
PLANE_T = 2 * 8 * KV_T + 1


def ring(n, k):
    return [(i, (i + k) % n) for i in range(n)]


def sum_of_squares(kv_grad, exp_grad):
    def kernel(kv_ref, exp_ref, out_ref):
        total = jnp.zeros((8, LANES), jnp.float32)
        for i in range(2):
            g = kv_ref[i, 0]
            total += jnp.sum((g * g).reshape(BLK // 8, 8, LANES), axis=0)
        for e in range(EXPERTS):
            for j in range(3):
                g = exp_ref[e, 0, j]
                total += jnp.sum((g * g).reshape(BLK // 8, 8, LANES), axis=0)
        out_ref[...] = total

    return pl.pallas_call(
        kernel,
        out_shape=jax.ShapeDtypeStruct((8, LANES), jnp.float32),
        in_specs=[pl.BlockSpec(memory_space=VMEM)] * 2,
        out_specs=pl.BlockSpec(memory_space=VMEM),
        name="sum_of_squares",
    )(kv_grad, exp_grad)


def sum_over_devices(v):
    for axis in ("x", "z"):
        others = [lax.ppermute(v, axis, ring(4, k)) for k in (1, 2, 3)]
        v = v + others[0] + others[1] + others[2]
    for pairs in ([(0, 2), (2, 0), (1, 3), (3, 1)], [(2, 1), (1, 2), (3, 0), (0, 3)]):
        v = v + lax.ppermute(v, ("yl", "yh"), pairs)
    v = v + lax.ppermute(v, "c", ring(2, 1))
    return v


def adam(master, gradient, moment_one, moment_two, factor):
    scaled = factor * gradient
    mean_new = beta_one * moment_one + (1.0 - beta_one) * scaled
    square_new = beta_two * moment_two + (1.0 - beta_two) * scaled * scaled
    corr_one = 1.0 - beta_one**step_count
    corr_two = 1.0 - beta_two**step_count
    update = mean_new / corr_one / (jnp.sqrt(square_new / corr_two) + adam_eps)
    return master - learn_rate * (update + decay_rate * master)


def slot_of(owner, shard, slot):
    chosen = jnp.int32(0)
    occupied = jnp.int32(0)
    for e in range(EXPERTS):
        rank = jnp.int32(0)
        for f in range(e):
            rank += (owner[f] == owner[e]).astype(jnp.int32)
        matched = jnp.logical_and(owner[e] == shard, rank == slot).astype(jnp.int32)
        chosen += matched * e
        occupied += matched
    return chosen, occupied


def update(place, owner, total, kv, exp):
    def kernel(place_ref, owner_ref, total_ref, *refs):
        kv_hbm, exp_hbm = refs[0:4], refs[4:8]
        kv_new, exp_new = refs[8:10]
        parts, kv_part = refs[10:14], refs[14]
        kv_in, exp_in, values, tiles, sems = refs[15:]
        kv_copies = [
            pltpu.make_async_copy(kv_hbm[a], kv_in.at[a], sems.at[EXPERTS, a]) for a in range(4)
        ]
        exp_copies = [
            [
                pltpu.make_async_copy(exp_hbm[a].at[e, 0], exp_in.at[a, e], sems.at[e, a])
                for a in range(4)
            ]
            for e in range(EXPERTS)
        ]
        for copies in [kv_copies] + exp_copies:
            for copy in copies:
                copy.start()
        norm = jnp.sqrt(jnp.sum(total_ref[...], keepdims=True)) + 1e-06
        factor = jnp.minimum(1.0, clip_norm / norm)
        row = lax.broadcasted_iota(jnp.int32, (TILE, LANES), 0)
        flat = row * LANES + lax.broadcasted_iota(jnp.int32, (TILE, LANES), 1)

        def block(ins, at):
            new = adam(ins[0, *at], ins[1, *at], ins[2, *at], ins[3, *at], factor)
            weights = new.astype(jnp.bfloat16).astype(jnp.float32)
            magnitude = jnp.max(jnp.abs(weights), keepdims=True)
            scaled = weights / (magnitude + scale_eps)
            return new, scaled.reshape(BLK // TILE, TILE, LANES).astype(jnp.bfloat16), magnitude

        for copy in kv_copies:
            copy.wait()
        place = place_ref[0]
        shard = lax.rem(place, 4)
        kv_tile = jnp.zeros((TILE, LANES), jnp.float32)
        for i in range(2):
            new, val, magnitude = block(kv_in, (i, 0))
            kv_new[i, 0] = new
            kv_part[8 * i : 8 * i + 8] = val
            kv_tile = jnp.where(flat == i * LANES + place, magnitude, kv_tile)
        kv_part[16] = kv_tile.astype(jnp.bfloat16)
        for e in range(EXPERTS):
            for copy in exp_copies[e]:
                copy.wait()
            tile = jnp.zeros((TILE, LANES), jnp.float32)
            for j in range(3):
                new, val, magnitude = block(exp_in, (e, j))
                exp_new[e, 0, j] = new
                values[e, 8 * j : 8 * j + 8] = val
                at = place * 3 + j
                here = jnp.logical_or(flat == at, flat == at + 2 * LANES)
                tile = jnp.where(here, magnitude, tile)
            tiles[e] = tile
        owners = [owner_ref[e] for e in range(EXPERTS)]
        for k in range(4):
            scales = jnp.zeros((TILE, LANES), jnp.float32)
            for h in range(SLOTS):
                chosen, occupied = slot_of(owners, lax.rem(shard + k, 4), h)
                picked = values[chosen]
                at = 1 + h * SLOT_T
                parts[k][at : at + SLOT_T] = jnp.where(
                    occupied > 0, picked, jnp.zeros_like(picked)
                )
                held = jnp.logical_and(lax.div(row, 2) == h, occupied > 0)
                scales = jnp.where(held, tiles[chosen], scales)
            parts[k][0] = scales.astype(jnp.bfloat16)

    f32, bf16 = jnp.float32, jnp.bfloat16
    return pl.pallas_call(
        kernel,
        out_shape=(
            jax.ShapeDtypeStruct((2, 1, BLK, BLK), f32),
            jax.ShapeDtypeStruct((EXPERTS, 1, 3, BLK, BLK), f32),
        )
        + (jax.ShapeDtypeStruct((PART_T, TILE, LANES), bf16),) * 4
        + (jax.ShapeDtypeStruct((17, TILE, LANES), bf16),),
        in_specs=[pl.BlockSpec(memory_space=SMEM)] * 2
        + [pl.BlockSpec(memory_space=VMEM)]
        + [pl.BlockSpec(memory_space=pltpu.HBM)] * 8,
        out_specs=[pl.BlockSpec(memory_space=VMEM)] * 7,
        scratch_shapes=[
            pltpu.VMEM((4, 2, 1, BLK, BLK), f32),
            pltpu.VMEM((4, EXPERTS, 3, BLK, BLK), f32),
            pltpu.VMEM((EXPERTS, SLOT_T, TILE, LANES), bf16),
            pltpu.VMEM((EXPERTS, TILE, LANES), f32),
            pltpu.SemaphoreType.DMA((EXPERTS + 1, 4)),
        ],
        compiler_params=pltpu.CompilerParams(vmem_limit_bytes=60 * 1024 * 1024),
        name="update",
    )(place, owner, total, *kv, *exp)


def join(place, parts):
    def kernel(place_ref, *refs):
        out = refs[4]
        shard = lax.rem(place_ref[0], 4)
        tile = jnp.zeros((TILE, LANES), jnp.float32)
        for k in range(4):
            z = lax.rem(shard - k + 4, 4)
            tile += refs[k][0].astype(jnp.float32)
            for h in range(SLOTS):
                got = refs[k][1 + h * SLOT_T : 1 + (h + 1) * SLOT_T]
                out[pl.ds(1 + 4 * h * SLOT_T + z * SLOT_T, SLOT_T)] = got
        out[0] = tile.astype(jnp.bfloat16)

    return pl.pallas_call(
        kernel,
        out_shape=jax.ShapeDtypeStruct((FULL_T, TILE, LANES), jnp.bfloat16),
        in_specs=[pl.BlockSpec(memory_space=SMEM)] + [pl.BlockSpec(memory_space=VMEM)] * 4,
        out_specs=pl.BlockSpec(memory_space=VMEM),
        compiler_params=pltpu.CompilerParams(vmem_limit_bytes=16 * 1024 * 1024),
        name="join",
    )(place, *parts)


def join_kv(place, parts):
    def kernel(place_ref, *refs):
        out = refs[5]
        replica = lax.div(place_ref[0], 4)
        y = lax.rem(lax.div(replica, 2), 2)
        views = [(refs[0], 0, y), (refs[1], 0, 1 - y)]
        for k in (1, 2, 3):
            views += [(refs[k + 1].at[0], k, y), (refs[k + 1].at[1], k, 1 - y)]
        tile = jnp.zeros((TILE, LANES), jnp.float32)
        for ref, steps, at_y in views:
            chip = chip_along(replica, steps) * 2 + at_y
            for h in range(2):
                out[pl.ds(KV_T * (8 * h + chip), KV_T)] = ref[KV_T * h : KV_T * (h + 1)]
            tile += ref[16].astype(jnp.float32)
        out[PLANE_T - 1] = tile.astype(jnp.bfloat16)

    return pl.pallas_call(
        kernel,
        out_shape=jax.ShapeDtypeStruct((PLANE_T, TILE, LANES), jnp.bfloat16),
        in_specs=[pl.BlockSpec(memory_space=SMEM)] + [pl.BlockSpec(memory_space=VMEM)] * 5,
        out_specs=pl.BlockSpec(memory_space=VMEM),
        compiler_params=pltpu.CompilerParams(vmem_limit_bytes=16 * 1024 * 1024),
        name="join_kv",
    )(place, *parts)


def chip_along(replica, steps):
    x, c = lax.div(replica, 4), lax.rem(replica, 2)
    return lax.rem(x + 4 + jnp.where(c == 0, -steps, steps), 4)


EXP_OUT = jax.ShapeDtypeStruct((SLOTS, 16 * 4 * SLOT_T, TILE, LANES), jnp.bfloat16)
KV_OUT = jax.ShapeDtypeStruct((2, 8, 2, 4, KV_T, TILE, LANES), jnp.bfloat16)


SIZE = {"P": FULL_T, "A": A_T, "B": FULL_T - A_T, "K": PLANE_T}
SCALES = {"P": 0, "A": 0, "K": PLANE_T - 1}


def lay(place, own, got, outs=None, pack=False, last=False):
    views = [(n, 0, piece, False) for n, (_, piece) in enumerate(own)]
    for n, (_, held) in enumerate(got):
        at = 0
        for piece in held:
            views.append((len(own) + n, at, piece, True))
            at += SIZE[piece[0]]
    arrays = [array for array, _ in own + got]
    total = sum(SIZE[piece[0]] for _, piece in own)
    with_scales = [view for view in views if view[2][0] != "B"]
    count = 2 * len(views) + (len(own) if pack else 0)

    def kernel(place_ref, *refs):
        ins = refs[: len(arrays)]
        sum_in = refs[len(arrays) + 2] if outs else None
        rest = refs[len(arrays) + (3 if outs else 0) :]
        exp_out, kv_out, results = rest[0], rest[1], rest[2:-3]
        tiles, tile_sems, sems = rest[-3:]
        here = place_ref[0]
        replica, shard = lax.div(here, 4), lax.rem(here, 4)
        copies, gets = [], []

        def copy(src, dst):
            copies.append(pltpu.make_async_copy(src, dst, sems.at[len(copies)]))
            copies[-1].start()

        for i, (n, at, piece, _) in enumerate(with_scales):
            src = ins[n].at[at + SCALES[piece[0]]]
            gets.append(pltpu.make_async_copy(src, tiles.at[i], tile_sems.at[i]))
            gets[-1].start()
        if pack:
            at = 0
            for n, (_, piece) in enumerate(own):
                copy(ins[n], results[1].at[pl.ds(at, SIZE[piece[0]])])
                at += SIZE[piece[0]]
        for n, base, (kind, steps, over_y), over_c in views:
            ref = ins[n]
            c = lax.rem(replica, 2)
            if over_c:
                c = 1 - c
            forward = jnp.where(c == 0, -steps, steps)
            if kind == "K":
                z = lax.rem(shard + 4 + forward, 4)
                for h in range(2):
                    blocks = ref.at[pl.ds(base + 8 * KV_T * h, 8 * KV_T)]
                    copy(blocks.reshape(8, KV_T, TILE, LANES), kv_out.at[h, :, c, z])
                continue
            y = lax.rem(lax.div(replica, 2), 2)
            if over_y:
                y = 1 - y
            x = lax.rem(lax.div(replica, 4) + 4 + forward, 4)
            n = 4 * SLOT_T
            to = (x * 4 + y * 2 + c) * n
            first = A_T - 1 - n
            if kind in "PA":
                copy(ref.at[pl.ds(base + 1, n)], exp_out.at[0, pl.ds(to, n)])
            if kind == "P":
                copy(ref.at[pl.ds(base + 1 + n, n)], exp_out.at[1, pl.ds(to, n)])
            if kind == "A":
                copy(ref.at[pl.ds(base + 1 + n, first)], exp_out.at[1, pl.ds(to, first)])
            if kind == "B":
                copy(ref.at[pl.ds(base, n - first)], exp_out.at[1, pl.ds(to + first, n - first)])
        for get in gets:
            get.wait()
        sums = [jnp.zeros((TILE, LANES), jnp.float32) for _ in range(2)]
        if outs:
            sums = [sum_in[0], sum_in[1]]
        for i, (_, _, piece, _) in enumerate(with_scales):
            sums[piece[0] == "K"] += tiles[i].astype(jnp.float32)
        if last:
            results[0][0] = sums[0][0:2]
            results[0][1] = sums[0][2:4]
            results[1][...] = sums[1][0:2]
        else:
            results[0][0] = sums[0]
            results[0][1] = sums[1]
        for c in copies:
            c.wait()

    out_shape = [EXP_OUT, KV_OUT]
    out_specs = [pl.BlockSpec(memory_space=pl.ANY)] * 2
    if last:
        out_shape += [
            jax.ShapeDtypeStruct((SLOTS, 2, LANES), jnp.float32),
            jax.ShapeDtypeStruct((2, LANES), jnp.float32),
        ]
        out_specs += [pl.BlockSpec(memory_space=VMEM)] * 2
    else:
        out_shape += [jax.ShapeDtypeStruct((2, TILE, LANES), jnp.float32)]
        out_specs += [pl.BlockSpec(memory_space=VMEM)]
    if pack:
        out_shape += [jax.ShapeDtypeStruct((total, TILE, LANES), jnp.bfloat16)]
        out_specs += [pl.BlockSpec(memory_space=pltpu.HBM)]
    first_out = 1 + len(arrays)
    return pl.pallas_call(
        kernel,
        out_shape=tuple(out_shape),
        in_specs=[pl.BlockSpec(memory_space=SMEM)]
        + [pl.BlockSpec(memory_space=pl.ANY)] * (len(arrays) + (2 if outs else 0))
        + [pl.BlockSpec(memory_space=VMEM)] * (1 if outs else 0),
        out_specs=tuple(out_specs),
        scratch_shapes=[
            pltpu.VMEM((len(with_scales), TILE, LANES), jnp.bfloat16),
            pltpu.SemaphoreType.DMA((len(with_scales),)),
            pltpu.SemaphoreType.DMA((count,)),
        ],
        input_output_aliases={first_out: 0, first_out + 1: 1} if outs else {},
        compiler_params=pltpu.CompilerParams(vmem_limit_bytes=4 * 1024 * 1024),
        cost_estimate=pl.CostEstimate(flops=0, transcendentals=0, bytes_accessed=count * 2**19),
        name="lay",
    )(place, *arrays, *(outs or []))


def after(*values):
    return lax.optimization_barrier(values)


def swap_core(v):
    return lax.ppermute(v, "c", ring(2, 1))


def swap_y(v):
    return lax.ppermute(v, "yl", ring(2, 1))


def along_x(v, k=1):
    step = (k, 4 - k)
    pairs = [(2 * x + c, 2 * ((x + step[c]) % 4) + c) for x in range(4) for c in range(2)]
    return lax.ppermute(v, ("x", "c"), pairs)


def along_z(v, k=1):
    step = (k, 4 - k)
    pairs = [(4 * c + z, 4 * c + (z + step[c]) % 4) for c in range(2) for z in range(4)]
    return lax.ppermute(v, ("c", "z"), pairs)


def per_device(
    kv_param, kv_grad, kv_mean, kv_square, exp_param, exp_grad, exp_mean, exp_square, expert_owner
):
    total = sum_over_devices(sum_of_squares(kv_grad, exp_grad))
    place = lax.axis_index(SHARD).astype(jnp.int32).reshape(1)
    kv_new, exp_new, *parts, kv_part = update(
        place,
        expert_owner,
        total,
        (kv_param, kv_grad, kv_mean, kv_square),
        (exp_param, exp_grad, exp_mean, exp_square),
    )
    parts = [parts[0]] + [lax.ppermute(parts[k], "z", ring(4, k)) for k in (1, 2, 3)]
    kv_across = swap_y(kv_part)
    kv_two = jnp.stack([kv_part, kv_across])
    kv_far = [along_x(kv_two, k) for k in (1, 2, 3)]
    *parts, kv_part, kv_across, k1, k2, k3 = after(*parts, kv_part, kv_across, *kv_far)

    w0 = join_kv(place, (kv_part, kv_across, k1, k2, k3))
    p0 = join(place, parts)
    q0, p1, p3, w1, w3 = swap_y(p0), along_x(p0), along_x(p0, 3), along_z(w0), along_z(w0, 3)
    q0, p1, p3, w1, w3 = after(q0, p1, p3, w1, w3)

    b1, b3, p2 = swap_y(p1[A_T:FULL_T]), swap_y(p3[A_T:FULL_T]), along_x(p1)
    qa = q0[0:A_T]
    a1, a3 = along_x(qa), along_x(qa, 3)
    held1 = [("P", 0, False), ("P", 1, False), ("P", 3, False), ("P", 0, True)]
    held1 += [("K", 0, False), ("K", 1, False), ("K", 3, False)]
    *outs, pack1 = lay(place, list(zip([p0, p1, p3, q0, w0, w1, w3], held1)), [], pack=True)
    a1, a3, b1, b3, p2, pack1, *outs = after(a1, a3, b1, b3, p2, pack1, *outs)

    b2, a2, w2 = swap_y(p2[A_T:FULL_T]), along_x(a1), along_z(w1)
    got1 = swap_core(pack1)
    held2 = [("A", 1, True), ("A", 3, True), ("B", 1, True), ("B", 3, True), ("P", 2, False)]
    *outs, pack2 = lay(place, list(zip([a1, a3, b1, b3, p2], held2)), [], outs, pack=True)
    a2, b2, w2, got1, pack2, *outs = after(a2, b2, w2, got1, pack2, *outs)

    held3 = [("A", 2, True), ("B", 2, True), ("K", 2, False)]
    own = [a2, b2, w2]
    got = [(swap_core(pack2), held2)] + [(swap_core(v), [p]) for v, p in zip(own, held3)]
    outs = lay(place, list(zip(own, held3)), [(got1, held1)], outs)
    exp_rollout, kv_rollout, exp_scales, kv_scales = lay(place, [], got, outs, last=True)
    return (
        kv_new,
        exp_new,
        kv_rollout.reshape(2, 64, BLK, BLK),
        kv_scales[:, 0:64],
        exp_rollout.reshape(SLOTS, 1, 192, BLK, BLK),
        exp_scales.reshape(SLOTS, 1, 2 * LANES)[:, :, 0:192],
    )


def solution(mesh):
    fine = Mesh(mesh.devices.reshape(4, 2, 2, 4, 2), ("x", "yl", "c", "z", "yh"))
    kv = P("yh", SHARD, None, None)
    exp = P(None, "yh", SHARD, None, None)
    return jax.shard_map(
        per_device,
        mesh=fine,
        in_specs=(kv, kv, kv, kv, exp, exp, exp, exp, P()),
        out_specs=(
            kv,
            exp,
            P("yh", None, None, None),
            P("yh", None),
            P("z", "yh", None, None, None),
            P("z", "yh", None),
        ),
        check_vma=False,
    )
```

```python
import jax
import jax.numpy as jnp
from jax import lax
from jax.experimental import pallas as pl
from jax.experimental.pallas import tpu as pltpu
from jax.sharding import Mesh, PartitionSpec as P

SLOTS = 2
EXPERTS = 4
BLK = 128
LANES = 128

beta_one = 0.9
beta_two = 0.95
learn_rate = 0.25
decay_rate = 0.01
adam_eps = 1e-08
step_count = 20.0
clip_norm = 1.0
scale_eps = 1e-06

REPLICA = ("x", "yl", "c")
SHARD = ("x", "yl", "c", "z")
VMEM = pltpu.VMEM
SMEM = pltpu.SMEM

TILE = 16
SLOT_T = 24
PART_T = 1 + 2 * SLOT_T
FULL_T = 1 + 8 * SLOT_T
A_T = 129
KV_T = 8
PLANE_T = 2 * 8 * KV_T + 1


def ring(n, k):
    return [(i, (i + k) % n) for i in range(n)]


def sum_of_squares(kv_grad, exp_grad):
    def kernel(kv_ref, exp_ref, out_ref):
        total = jnp.zeros((8, LANES), jnp.float32)
        for i in range(2):
            g = kv_ref[i, 0]
            total += jnp.sum((g * g).reshape(BLK // 8, 8, LANES), axis=0)
        for e in range(EXPERTS):
            for j in range(3):
                g = exp_ref[e, 0, j]
                total += jnp.sum((g * g).reshape(BLK // 8, 8, LANES), axis=0)
        out_ref[...] = total

    return pl.pallas_call(
        kernel,
        out_shape=jax.ShapeDtypeStruct((8, LANES), jnp.float32),
        in_specs=[pl.BlockSpec(memory_space=VMEM)] * 2,
        out_specs=pl.BlockSpec(memory_space=VMEM),
        name="sum_of_squares",
    )(kv_grad, exp_grad)


def sum_over_devices(v):
    for axis in ("x", "z"):
        others = [lax.ppermute(v, axis, ring(4, k)) for k in (1, 2, 3)]
        v = v + others[0] + others[1] + others[2]
    for pairs in ([(0, 2), (2, 0), (1, 3), (3, 1)], [(2, 1), (1, 2), (3, 0), (0, 3)]):
        v = v + lax.ppermute(v, ("yl", "yh"), pairs)
    v = v + lax.ppermute(v, "c", ring(2, 1))
    return v


def adam(master, gradient, moment_one, moment_two, factor):
    scaled = factor * gradient
    mean_new = beta_one * moment_one + (1.0 - beta_one) * scaled
    square_new = beta_two * moment_two + (1.0 - beta_two) * scaled * scaled
    corr_one = 1.0 - beta_one**step_count
    corr_two = 1.0 - beta_two**step_count
    update = mean_new / corr_one / (jnp.sqrt(square_new / corr_two) + adam_eps)
    return master - learn_rate * (update + decay_rate * master)


def slot_of(owner, shard, slot):
    chosen = jnp.int32(0)
    occupied = jnp.int32(0)
    for e in range(EXPERTS):
        rank = jnp.int32(0)
        for f in range(e):
            rank += (owner[f] == owner[e]).astype(jnp.int32)
        matched = jnp.logical_and(owner[e] == shard, rank == slot).astype(jnp.int32)
        chosen += matched * e
        occupied += matched
    return chosen, occupied


def update(place, owner, total, kv, exp):
    def kernel(place_ref, owner_ref, total_ref, *refs):
        kv_hbm, exp_hbm = refs[0:4], refs[4:8]
        kv_new, exp_new = refs[8:10]
        parts, kv_part = refs[10:14], refs[14]
        kv_in, exp_in, values, tiles, sems = refs[15:]
        kv_copies = [
            pltpu.make_async_copy(kv_hbm[a], kv_in.at[a], sems.at[EXPERTS, a]) for a in range(4)
        ]
        exp_copies = [
            [
                pltpu.make_async_copy(exp_hbm[a].at[e, 0], exp_in.at[a, e], sems.at[e, a])
                for a in range(4)
            ]
            for e in range(EXPERTS)
        ]
        for copies in [kv_copies] + exp_copies:
            for copy in copies:
                copy.start()
        norm = jnp.sqrt(jnp.sum(total_ref[...], keepdims=True)) + 1e-06
        factor = jnp.minimum(1.0, clip_norm / norm)
        row = lax.broadcasted_iota(jnp.int32, (TILE, LANES), 0)
        flat = row * LANES + lax.broadcasted_iota(jnp.int32, (TILE, LANES), 1)

        def block(ins, at):
            new = adam(ins[0, *at], ins[1, *at], ins[2, *at], ins[3, *at], factor)
            weights = new.astype(jnp.bfloat16).astype(jnp.float32)
            magnitude = jnp.max(jnp.abs(weights), keepdims=True)
            scaled = weights / (magnitude + scale_eps)
            return new, scaled.reshape(BLK // TILE, TILE, LANES).astype(jnp.bfloat16), magnitude

        for copy in kv_copies:
            copy.wait()
        place = place_ref[0]
        shard = lax.rem(place, 4)
        kv_tile = jnp.zeros((TILE, LANES), jnp.float32)
        for i in range(2):
            new, val, magnitude = block(kv_in, (i, 0))
            kv_new[i, 0] = new
            kv_part[8 * i : 8 * i + 8] = val
            kv_tile = jnp.where(flat == i * LANES + place, magnitude, kv_tile)
        kv_part[16] = kv_tile.astype(jnp.bfloat16)
        for e in range(EXPERTS):
            for copy in exp_copies[e]:
                copy.wait()
            tile = jnp.zeros((TILE, LANES), jnp.float32)
            for j in range(3):
                new, val, magnitude = block(exp_in, (e, j))
                exp_new[e, 0, j] = new
                values[e, 8 * j : 8 * j + 8] = val
                at = place * 3 + j
                here = jnp.logical_or(flat == at, flat == at + 2 * LANES)
                tile = jnp.where(here, magnitude, tile)
            tiles[e] = tile
        owners = [owner_ref[e] for e in range(EXPERTS)]
        for k in range(4):
            scales = jnp.zeros((TILE, LANES), jnp.float32)
            for h in range(SLOTS):
                chosen, occupied = slot_of(owners, lax.rem(shard + k, 4), h)
                picked = values[chosen]
                at = 1 + h * SLOT_T
                parts[k][at : at + SLOT_T] = jnp.where(
                    occupied > 0, picked, jnp.zeros_like(picked)
                )
                held = jnp.logical_and(lax.div(row, 2) == h, occupied > 0)
                scales = jnp.where(held, tiles[chosen], scales)
            parts[k][0] = scales.astype(jnp.bfloat16)

    f32, bf16 = jnp.float32, jnp.bfloat16
    return pl.pallas_call(
        kernel,
        out_shape=(
            jax.ShapeDtypeStruct((2, 1, BLK, BLK), f32),
            jax.ShapeDtypeStruct((EXPERTS, 1, 3, BLK, BLK), f32),
        )
        + (jax.ShapeDtypeStruct((PART_T, TILE, LANES), bf16),) * 4
        + (jax.ShapeDtypeStruct((17, TILE, LANES), bf16),),
        in_specs=[pl.BlockSpec(memory_space=SMEM)] * 2
        + [pl.BlockSpec(memory_space=VMEM)]
        + [pl.BlockSpec(memory_space=pltpu.HBM)] * 8,
        out_specs=[pl.BlockSpec(memory_space=VMEM)] * 7,
        scratch_shapes=[
            pltpu.VMEM((4, 2, 1, BLK, BLK), f32),
            pltpu.VMEM((4, EXPERTS, 3, BLK, BLK), f32),
            pltpu.VMEM((EXPERTS, SLOT_T, TILE, LANES), bf16),
            pltpu.VMEM((EXPERTS, TILE, LANES), f32),
            pltpu.SemaphoreType.DMA((EXPERTS + 1, 4)),
        ],
        compiler_params=pltpu.CompilerParams(vmem_limit_bytes=60 * 1024 * 1024),
        name="update",
    )(place, owner, total, *kv, *exp)


def join(place, parts):
    def kernel(place_ref, *refs):
        out = refs[4]
        shard = lax.rem(place_ref[0], 4)
        tile = jnp.zeros((TILE, LANES), jnp.float32)
        for k in range(4):
            z = lax.rem(shard - k + 4, 4)
            tile += refs[k][0].astype(jnp.float32)
            for h in range(SLOTS):
                got = refs[k][1 + h * SLOT_T : 1 + (h + 1) * SLOT_T]
                out[pl.ds(1 + 4 * h * SLOT_T + z * SLOT_T, SLOT_T)] = got
        out[0] = tile.astype(jnp.bfloat16)

    return pl.pallas_call(
        kernel,
        out_shape=jax.ShapeDtypeStruct((FULL_T, TILE, LANES), jnp.bfloat16),
        in_specs=[pl.BlockSpec(memory_space=SMEM)] + [pl.BlockSpec(memory_space=VMEM)] * 4,
        out_specs=pl.BlockSpec(memory_space=VMEM),
        compiler_params=pltpu.CompilerParams(vmem_limit_bytes=16 * 1024 * 1024),
        name="join",
    )(place, *parts)


def join_kv(place, parts):
    def kernel(place_ref, *refs):
        out = refs[5]
        replica = lax.div(place_ref[0], 4)
        y = lax.rem(lax.div(replica, 2), 2)
        views = [(refs[0], 0, y), (refs[1], 0, 1 - y)]
        for k in (1, 2, 3):
            views += [(refs[k + 1].at[0], k, y), (refs[k + 1].at[1], k, 1 - y)]
        tile = jnp.zeros((TILE, LANES), jnp.float32)
        for ref, steps, at_y in views:
            chip = chip_along(replica, steps) * 2 + at_y
            for h in range(2):
                out[pl.ds(KV_T * (8 * h + chip), KV_T)] = ref[KV_T * h : KV_T * (h + 1)]
            tile += ref[16].astype(jnp.float32)
        out[PLANE_T - 1] = tile.astype(jnp.bfloat16)

    return pl.pallas_call(
        kernel,
        out_shape=jax.ShapeDtypeStruct((PLANE_T, TILE, LANES), jnp.bfloat16),
        in_specs=[pl.BlockSpec(memory_space=SMEM)] + [pl.BlockSpec(memory_space=VMEM)] * 5,
        out_specs=pl.BlockSpec(memory_space=VMEM),
        compiler_params=pltpu.CompilerParams(vmem_limit_bytes=16 * 1024 * 1024),
        name="join_kv",
    )(place, *parts)


def chip_along(replica, steps):
    x, c = lax.div(replica, 4), lax.rem(replica, 2)
    return lax.rem(x + 4 + jnp.where(c == 0, -steps, steps), 4)


EXP_OUT = jax.ShapeDtypeStruct((SLOTS, 16 * 4 * SLOT_T, TILE, LANES), jnp.bfloat16)
KV_OUT = jax.ShapeDtypeStruct((2, 8, 2, 4, KV_T, TILE, LANES), jnp.bfloat16)


SIZE = {"P": FULL_T, "A": A_T, "B": FULL_T - A_T, "K": PLANE_T}
SCALES = {"P": 0, "A": 0, "K": PLANE_T - 1}


def lay(place, own, got, outs=None, pack=0, last=False):
    views = [(n, 0, piece, False) for n, (_, piece) in enumerate(own)]
    for n, (_, held) in enumerate(got):
        at = 0
        for piece in held:
            views.append((len(own) + n, at, piece, True))
            at += SIZE[piece[0]]
    arrays = [array for array, _ in own + got]
    total = sum(SIZE[piece[0]] for _, piece in own[:pack])
    with_scales = [view for view in views if view[2][0] != "B"]
    count = 2 * len(views) + pack

    def kernel(place_ref, *refs):
        ins = refs[: len(arrays)]
        sum_in = refs[len(arrays) + 2] if outs else None
        rest = refs[len(arrays) + (3 if outs else 0) :]
        exp_out, kv_out, results = rest[0], rest[1], rest[2:-3]
        tiles, tile_sems, sems = rest[-3:]
        here = place_ref[0]
        replica, shard = lax.div(here, 4), lax.rem(here, 4)
        copies, gets = [], []

        def copy(src, dst):
            copies.append(pltpu.make_async_copy(src, dst, sems.at[len(copies)]))
            copies[-1].start()

        for i, (n, at, piece, _) in enumerate(with_scales):
            src = ins[n].at[at + SCALES[piece[0]]]
            gets.append(pltpu.make_async_copy(src, tiles.at[i], tile_sems.at[i]))
            gets[-1].start()
        if pack:
            at = 0
            for n, (_, piece) in enumerate(own[:pack]):
                copy(ins[n], results[1].at[pl.ds(at, SIZE[piece[0]])])
                at += SIZE[piece[0]]
        for n, base, (kind, steps, over_y), over_c in views:
            ref = ins[n]
            c = lax.rem(replica, 2)
            if over_c:
                c = 1 - c
            forward = jnp.where(c == 0, -steps, steps)
            if kind == "K":
                z = lax.rem(shard + 4 + forward, 4)
                for h in range(2):
                    blocks = ref.at[pl.ds(base + 8 * KV_T * h, 8 * KV_T)]
                    copy(blocks.reshape(8, KV_T, TILE, LANES), kv_out.at[h, :, c, z])
                continue
            y = lax.rem(lax.div(replica, 2), 2)
            if over_y:
                y = 1 - y
            x = lax.rem(lax.div(replica, 4) + 4 + forward, 4)
            n = 4 * SLOT_T
            to = (x * 4 + y * 2 + c) * n
            first = A_T - 1 - n
            if kind in "PA":
                copy(ref.at[pl.ds(base + 1, n)], exp_out.at[0, pl.ds(to, n)])
            if kind == "P":
                copy(ref.at[pl.ds(base + 1 + n, n)], exp_out.at[1, pl.ds(to, n)])
            if kind == "A":
                copy(ref.at[pl.ds(base + 1 + n, first)], exp_out.at[1, pl.ds(to, first)])
            if kind == "B":
                copy(ref.at[pl.ds(base, n - first)], exp_out.at[1, pl.ds(to + first, n - first)])
        for get in gets:
            get.wait()
        sums = [jnp.zeros((TILE, LANES), jnp.float32) for _ in range(2)]
        if outs:
            sums = [sum_in[0], sum_in[1]]
        for i, (_, _, piece, _) in enumerate(with_scales):
            sums[piece[0] == "K"] += tiles[i].astype(jnp.float32)
        if last:
            results[0][0] = sums[0][0:2]
            results[0][1] = sums[0][2:4]
            results[1][...] = sums[1][0:2]
        else:
            results[0][0] = sums[0]
            results[0][1] = sums[1]
        for c in copies:
            c.wait()

    out_shape = [EXP_OUT, KV_OUT]
    out_specs = [pl.BlockSpec(memory_space=pl.ANY)] * 2
    if last:
        out_shape += [
            jax.ShapeDtypeStruct((SLOTS, 2, LANES), jnp.float32),
            jax.ShapeDtypeStruct((2, LANES), jnp.float32),
        ]
        out_specs += [pl.BlockSpec(memory_space=VMEM)] * 2
    else:
        out_shape += [jax.ShapeDtypeStruct((2, TILE, LANES), jnp.float32)]
        out_specs += [pl.BlockSpec(memory_space=VMEM)]
    if pack:
        out_shape += [jax.ShapeDtypeStruct((total, TILE, LANES), jnp.bfloat16)]
        out_specs += [pl.BlockSpec(memory_space=pltpu.HBM)]
    first_out = 1 + len(arrays)
    return pl.pallas_call(
        kernel,
        out_shape=tuple(out_shape),
        in_specs=[pl.BlockSpec(memory_space=SMEM)]
        + [pl.BlockSpec(memory_space=pl.ANY)] * (len(arrays) + (2 if outs else 0))
        + [pl.BlockSpec(memory_space=VMEM)] * (1 if outs else 0),
        out_specs=tuple(out_specs),
        scratch_shapes=[
            pltpu.VMEM((len(with_scales), TILE, LANES), jnp.bfloat16),
            pltpu.SemaphoreType.DMA((len(with_scales),)),
            pltpu.SemaphoreType.DMA((count,)),
        ],
        input_output_aliases={first_out: 0, first_out + 1: 1} if outs else {},
        compiler_params=pltpu.CompilerParams(vmem_limit_bytes=4 * 1024 * 1024),
        cost_estimate=pl.CostEstimate(flops=0, transcendentals=0, bytes_accessed=count * 2**19),
        name="lay",
    )(place, *arrays, *(outs or []))


def after(*values):
    return lax.optimization_barrier(values)


def swap_core(v):
    return lax.ppermute(v, "c", ring(2, 1))


def swap_y(v):
    return lax.ppermute(v, "yl", ring(2, 1))


def along_x(v, k=1):
    step = (k, 4 - k)
    pairs = [(2 * x + c, 2 * ((x + step[c]) % 4) + c) for x in range(4) for c in range(2)]
    return lax.ppermute(v, ("x", "c"), pairs)


def along_z(v, k=1):
    step = (k, 4 - k)
    pairs = [(4 * c + z, 4 * c + (z + step[c]) % 4) for c in range(2) for z in range(4)]
    return lax.ppermute(v, ("c", "z"), pairs)


def per_device(
    kv_param, kv_grad, kv_mean, kv_square, exp_param, exp_grad, exp_mean, exp_square, expert_owner
):
    total = sum_over_devices(sum_of_squares(kv_grad, exp_grad))
    place = lax.axis_index(SHARD).astype(jnp.int32).reshape(1)
    kv_new, exp_new, *parts, kv_part = update(
        place,
        expert_owner,
        total,
        (kv_param, kv_grad, kv_mean, kv_square),
        (exp_param, exp_grad, exp_mean, exp_square),
    )
    parts = [parts[0]] + [lax.ppermute(parts[k], "z", ring(4, k)) for k in (1, 2, 3)]
    kv_across = swap_y(kv_part)
    kv_two = jnp.stack([kv_part, kv_across])
    kv_far = [along_x(kv_two, k) for k in (1, 2, 3)]
    *parts, kv_part, kv_across, k1, k2, k3 = after(*parts, kv_part, kv_across, *kv_far)

    w0 = join_kv(place, (kv_part, kv_across, k1, k2, k3))
    p0 = join(place, parts)
    q0, p1, p3, w1, w3 = swap_y(p0), along_x(p0), along_x(p0, 3), along_z(w0), along_z(w0, 3)
    q0, p1, p3, w1, w3 = after(q0, p1, p3, w1, w3)

    b1, b3, p2 = swap_y(p1[A_T:FULL_T]), swap_y(p3[A_T:FULL_T]), along_x(p1)
    qa = q0[0:A_T]
    a1, a3 = along_x(qa), along_x(qa, 3)
    held1 = [("P", 0, False), ("P", 1, False), ("P", 3, False), ("P", 0, True)]
    held1 += [("K", 0, False), ("K", 1, False), ("K", 3, False)]
    *outs, pack1 = lay(place, list(zip([p0, p1, p3, q0, w0, w1, w3], held1)), [], pack=7)
    a1, a3, b1, b3, p2, pack1, *outs = after(a1, a3, b1, b3, p2, pack1, *outs)

    b2, a2, w2 = swap_y(p2[A_T:FULL_T]), along_x(a1), along_z(w1)
    got1, got_p2 = swap_core(pack1), swap_core(p2)
    held2 = [("A", 1, True), ("A", 3, True), ("B", 1, True), ("B", 3, True)]
    held_p2 = [("P", 2, False)]
    own = list(zip([a1, a3, b1, b3, p2], held2 + held_p2))
    *outs, pack2 = lay(place, own, [], outs, pack=4)
    a2, b2, w2, got1, got_p2, pack2, *outs = after(a2, b2, w2, got1, got_p2, pack2, *outs)

    held3 = [("A", 2, True), ("B", 2, True), ("K", 2, False)]
    own = [a2, b2, w2]
    got2 = swap_core(pack2)
    got3 = [(swap_core(v), [p]) for v, p in zip(own, held3)]
    outs = lay(place, list(zip(own, held3)), [(got1, held1), (got_p2, held_p2)], outs)
    outs = lay(place, [], [(got2, held2)], outs)
    exp_rollout, kv_rollout, exp_scales, kv_scales = lay(place, [], got3, outs, last=True)
    return (
        kv_new,
        exp_new,
        kv_rollout.reshape(2, 64, BLK, BLK),
        kv_scales[:, 0:64],
        exp_rollout.reshape(SLOTS, 1, 192, BLK, BLK),
        exp_scales.reshape(SLOTS, 1, 2 * LANES)[:, :, 0:192],
    )


def solution(mesh):
    fine = Mesh(mesh.devices.reshape(4, 2, 2, 4, 2), ("x", "yl", "c", "z", "yh"))
    kv = P("yh", SHARD, None, None)
    exp = P(None, "yh", SHARD, None, None)
    return jax.shard_map(
        per_device,
        mesh=fine,
        in_specs=(kv, kv, kv, kv, exp, exp, exp, exp, P()),
        out_specs=(
            kv,
            exp,
            P("yh", None, None, None),
            P("yh", None),
            P("z", "yh", None, None, None),
            P("z", "yh", None),
        ),
        check_vma=False,
    )
```

```python
import jax
import jax.numpy as jnp
from jax import lax
from jax.experimental import pallas as pl
from jax.experimental.pallas import tpu as pltpu
from jax.sharding import Mesh, PartitionSpec as P

SLOTS = 2
EXPERTS = 4
BLK = 128
LANES = 128

beta_one = 0.9
beta_two = 0.95
learn_rate = 0.25
decay_rate = 0.01
adam_eps = 1e-08
step_count = 20.0
clip_norm = 1.0
scale_eps = 1e-06

REPLICA = ("x", "yl", "c")
SHARD = ("x", "yl", "c", "z")
VMEM = pltpu.VMEM
SMEM = pltpu.SMEM

TILE = 16
SLOT_T = 24
PART_T = 1 + 2 * SLOT_T
FULL_T = 1 + 8 * SLOT_T
A_T = 113
KV_T = 8
PLANE_T = 2 * 8 * KV_T + 1


def ring(n, k):
    return [(i, (i + k) % n) for i in range(n)]


def sum_of_squares(kv_grad, exp_grad):
    def kernel(kv_ref, exp_ref, out_ref):
        total = jnp.zeros((8, LANES), jnp.float32)
        for i in range(2):
            g = kv_ref[i, 0]
            total += jnp.sum((g * g).reshape(BLK // 8, 8, LANES), axis=0)
        for e in range(EXPERTS):
            for j in range(3):
                g = exp_ref[e, 0, j]
                total += jnp.sum((g * g).reshape(BLK // 8, 8, LANES), axis=0)
        out_ref[...] = total

    return pl.pallas_call(
        kernel,
        out_shape=jax.ShapeDtypeStruct((8, LANES), jnp.float32),
        in_specs=[pl.BlockSpec(memory_space=VMEM)] * 2,
        out_specs=pl.BlockSpec(memory_space=VMEM),
        name="sum_of_squares",
    )(kv_grad, exp_grad)


def sum_over_devices(v):
    for along in (along_x, along_z):
        others = [along(v, k) for k in (1, 2, 3)]
        v = v + others[0] + others[1] + others[2]
    for pairs in ([(0, 2), (2, 0), (1, 3), (3, 1)], [(2, 1), (1, 2), (3, 0), (0, 3)]):
        v = v + lax.ppermute(v, ("yl", "yh"), pairs)
    v = v + lax.ppermute(v, "c", ring(2, 1))
    return v


def adam(master, gradient, moment_one, moment_two, factor):
    scaled = factor * gradient
    mean_new = beta_one * moment_one + (1.0 - beta_one) * scaled
    square_new = beta_two * moment_two + (1.0 - beta_two) * scaled * scaled
    corr_one = 1.0 - beta_one**step_count
    corr_two = 1.0 - beta_two**step_count
    update = mean_new / corr_one / (jnp.sqrt(square_new / corr_two) + adam_eps)
    return master - learn_rate * (update + decay_rate * master)


def slot_of(owner, shard, slot):
    chosen = jnp.int32(0)
    occupied = jnp.int32(0)
    for e in range(EXPERTS):
        rank = jnp.int32(0)
        for f in range(e):
            rank += (owner[f] == owner[e]).astype(jnp.int32)
        matched = jnp.logical_and(owner[e] == shard, rank == slot).astype(jnp.int32)
        chosen += matched * e
        occupied += matched
    return chosen, occupied


def update(place, owner, total, kv, exp):
    def kernel(place_ref, owner_ref, total_ref, *refs):
        kv_hbm, exp_hbm = refs[0:4], refs[4:8]
        kv_new, exp_new = refs[8:10]
        parts, kv_part = refs[10:14], refs[14]
        kv_in, exp_in, values, tiles, sems = refs[15:]
        kv_copies = [
            pltpu.make_async_copy(kv_hbm[a], kv_in.at[a], sems.at[EXPERTS, a]) for a in range(4)
        ]
        exp_copies = [
            [
                pltpu.make_async_copy(exp_hbm[a].at[e, 0], exp_in.at[a, e], sems.at[e, a])
                for a in range(4)
            ]
            for e in range(EXPERTS)
        ]
        for copies in [kv_copies] + exp_copies:
            for copy in copies:
                copy.start()
        norm = jnp.sqrt(jnp.sum(total_ref[...], keepdims=True)) + 1e-06
        factor = jnp.minimum(1.0, clip_norm / norm)
        row = lax.broadcasted_iota(jnp.int32, (TILE, LANES), 0)
        flat = row * LANES + lax.broadcasted_iota(jnp.int32, (TILE, LANES), 1)

        def block(ins, at):
            new = adam(ins[0, *at], ins[1, *at], ins[2, *at], ins[3, *at], factor)
            weights = new.astype(jnp.bfloat16).astype(jnp.float32)
            magnitude = jnp.max(jnp.abs(weights), keepdims=True)
            scaled = weights / (magnitude + scale_eps)
            return new, scaled.reshape(BLK // TILE, TILE, LANES).astype(jnp.bfloat16), magnitude

        for copy in kv_copies:
            copy.wait()
        place = place_ref[0]
        shard = lax.rem(place, 4)
        kv_tile = jnp.zeros((TILE, LANES), jnp.float32)
        for i in range(2):
            new, val, magnitude = block(kv_in, (i, 0))
            kv_new[i, 0] = new
            kv_part[8 * i : 8 * i + 8] = val
            kv_tile = jnp.where(flat == i * LANES + place, magnitude, kv_tile)
        kv_part[16] = kv_tile.astype(jnp.bfloat16)
        for e in range(EXPERTS):
            for copy in exp_copies[e]:
                copy.wait()
            tile = jnp.zeros((TILE, LANES), jnp.float32)
            for j in range(3):
                new, val, magnitude = block(exp_in, (e, j))
                exp_new[e, 0, j] = new
                values[e, 8 * j : 8 * j + 8] = val
                at = place * 3 + j
                here = jnp.logical_or(flat == at, flat == at + 2 * LANES)
                tile = jnp.where(here, magnitude, tile)
            tiles[e] = tile
        owners = [owner_ref[e] for e in range(EXPERTS)]
        for k in range(4):
            scales = jnp.zeros((TILE, LANES), jnp.float32)
            for h in range(SLOTS):
                chosen, occupied = slot_of(owners, lax.rem(shard + steps_of(place, k), 4), h)
                picked = values[chosen]
                at = 1 + h * SLOT_T
                parts[k][at : at + SLOT_T] = jnp.where(
                    occupied > 0, picked, jnp.zeros_like(picked)
                )
                held = jnp.logical_and(lax.div(row, 2) == h, occupied > 0)
                scales = jnp.where(held, tiles[chosen], scales)
            parts[k][0] = scales.astype(jnp.bfloat16)

    f32, bf16 = jnp.float32, jnp.bfloat16
    return pl.pallas_call(
        kernel,
        out_shape=(
            jax.ShapeDtypeStruct((2, 1, BLK, BLK), f32),
            jax.ShapeDtypeStruct((EXPERTS, 1, 3, BLK, BLK), f32),
        )
        + (jax.ShapeDtypeStruct((PART_T, TILE, LANES), bf16),) * 4
        + (jax.ShapeDtypeStruct((17, TILE, LANES), bf16),),
        in_specs=[pl.BlockSpec(memory_space=SMEM)] * 2
        + [pl.BlockSpec(memory_space=VMEM)]
        + [pl.BlockSpec(memory_space=pltpu.HBM)] * 8,
        out_specs=[pl.BlockSpec(memory_space=VMEM)] * 7,
        scratch_shapes=[
            pltpu.VMEM((4, 2, 1, BLK, BLK), f32),
            pltpu.VMEM((4, EXPERTS, 3, BLK, BLK), f32),
            pltpu.VMEM((EXPERTS, SLOT_T, TILE, LANES), bf16),
            pltpu.VMEM((EXPERTS, TILE, LANES), f32),
            pltpu.SemaphoreType.DMA((EXPERTS + 1, 4)),
        ],
        compiler_params=pltpu.CompilerParams(vmem_limit_bytes=60 * 1024 * 1024),
        name="update",
    )(place, owner, total, *kv, *exp)


def steps_of(place, k):
    core = lax.rem(lax.div(place, 4), 2)
    return jnp.where(core == 0, k, (4 - k) % 4)


def join(place, parts):
    def kernel(place_ref, *refs):
        out = refs[4]
        shard = lax.rem(place_ref[0], 4)
        tile = jnp.zeros((TILE, LANES), jnp.float32)
        for k in range(4):
            z = lax.rem(shard - steps_of(place_ref[0], k) + 4, 4)
            tile += refs[k][0].astype(jnp.float32)
            for h in range(SLOTS):
                got = refs[k][1 + h * SLOT_T : 1 + (h + 1) * SLOT_T]
                out[pl.ds(1 + 4 * h * SLOT_T + z * SLOT_T, SLOT_T)] = got
        out[0] = tile.astype(jnp.bfloat16)

    return pl.pallas_call(
        kernel,
        out_shape=jax.ShapeDtypeStruct((FULL_T, TILE, LANES), jnp.bfloat16),
        in_specs=[pl.BlockSpec(memory_space=SMEM)] + [pl.BlockSpec(memory_space=VMEM)] * 4,
        out_specs=pl.BlockSpec(memory_space=VMEM),
        compiler_params=pltpu.CompilerParams(vmem_limit_bytes=16 * 1024 * 1024),
        name="join",
    )(place, *parts)


def join_kv(place, parts):
    def kernel(place_ref, *refs):
        out = refs[5]
        replica = lax.div(place_ref[0], 4)
        y = lax.rem(lax.div(replica, 2), 2)
        views = [(refs[0], 0, y), (refs[1], 0, 1 - y)]
        for k in (1, 2, 3):
            views += [(refs[k + 1].at[0], k, y), (refs[k + 1].at[1], k, 1 - y)]
        tile = jnp.zeros((TILE, LANES), jnp.float32)
        for ref, steps, at_y in views:
            chip = chip_along(replica, steps) * 2 + at_y
            for h in range(2):
                out[pl.ds(KV_T * (8 * h + chip), KV_T)] = ref[KV_T * h : KV_T * (h + 1)]
            tile += ref[16].astype(jnp.float32)
        out[PLANE_T - 1] = tile.astype(jnp.bfloat16)

    return pl.pallas_call(
        kernel,
        out_shape=jax.ShapeDtypeStruct((PLANE_T, TILE, LANES), jnp.bfloat16),
        in_specs=[pl.BlockSpec(memory_space=SMEM)] + [pl.BlockSpec(memory_space=VMEM)] * 5,
        out_specs=pl.BlockSpec(memory_space=VMEM),
        compiler_params=pltpu.CompilerParams(vmem_limit_bytes=16 * 1024 * 1024),
        name="join_kv",
    )(place, *parts)


def chip_along(replica, steps):
    x, c = lax.div(replica, 4), lax.rem(replica, 2)
    return lax.rem(x + 4 + jnp.where(c == 0, -steps, steps), 4)


EXP_OUT = jax.ShapeDtypeStruct((SLOTS, 16 * 4 * SLOT_T, TILE, LANES), jnp.bfloat16)
KV_OUT = jax.ShapeDtypeStruct((2, 8, 2, 4, KV_T, TILE, LANES), jnp.bfloat16)


SIZE = {"P": FULL_T, "A": A_T, "B": FULL_T - A_T, "K": PLANE_T}
SCALES = {"P": 0, "A": 0, "K": PLANE_T - 1}


def lay(place, own, got, outs=None, pack=0, last=False):
    views = [(n, 0, piece, False) for n, (_, piece) in enumerate(own)]
    for n, (_, held) in enumerate(got):
        at = 0
        for piece in held:
            views.append((len(own) + n, at, piece, True))
            at += SIZE[piece[0]]
    arrays = [array for array, _ in own + got]
    total = sum(SIZE[piece[0]] for _, piece in own[:pack])
    with_scales = [view for view in views if view[2][0] != "B"]
    count = 2 * len(views) + pack

    def kernel(place_ref, *refs):
        ins = refs[: len(arrays)]
        sum_in = refs[len(arrays) + 2] if outs else None
        rest = refs[len(arrays) + (3 if outs else 0) :]
        exp_out, kv_out, results = rest[0], rest[1], rest[2:-3]
        tiles, tile_sems, sems = rest[-3:]
        here = place_ref[0]
        replica, shard = lax.div(here, 4), lax.rem(here, 4)
        copies, gets = [], []

        def copy(src, dst):
            copies.append(pltpu.make_async_copy(src, dst, sems.at[len(copies)]))
            copies[-1].start()

        for i, (n, at, piece, _) in enumerate(with_scales):
            src = ins[n].at[at + SCALES[piece[0]]]
            gets.append(pltpu.make_async_copy(src, tiles.at[i], tile_sems.at[i]))
            gets[-1].start()
        if pack:
            at = 0
            for n, (_, piece) in enumerate(own[:pack]):
                copy(ins[n], results[1].at[pl.ds(at, SIZE[piece[0]])])
                at += SIZE[piece[0]]
        for n, base, (kind, steps, over_y), over_c in views:
            ref = ins[n]
            c = lax.rem(replica, 2)
            if over_c:
                c = 1 - c
            forward = jnp.where(c == 0, -steps, steps)
            if kind == "K":
                z = lax.rem(shard + 4 + forward, 4)
                for h in range(2):
                    blocks = ref.at[pl.ds(base + 8 * KV_T * h, 8 * KV_T)]
                    copy(blocks.reshape(8, KV_T, TILE, LANES), kv_out.at[h, :, c, z])
                continue
            y = lax.rem(lax.div(replica, 2), 2)
            if over_y:
                y = 1 - y
            x = lax.rem(lax.div(replica, 4) + 4 + forward, 4)
            n = 4 * SLOT_T
            to = (x * 4 + y * 2 + c) * n
            first = A_T - 1 - n
            if kind in "PA":
                copy(ref.at[pl.ds(base + 1, n)], exp_out.at[0, pl.ds(to, n)])
            if kind == "P":
                copy(ref.at[pl.ds(base + 1 + n, n)], exp_out.at[1, pl.ds(to, n)])
            if kind == "A":
                copy(ref.at[pl.ds(base + 1 + n, first)], exp_out.at[1, pl.ds(to, first)])
            if kind == "B":
                copy(ref.at[pl.ds(base, n - first)], exp_out.at[1, pl.ds(to + first, n - first)])
        for get in gets:
            get.wait()
        sums = [jnp.zeros((TILE, LANES), jnp.float32) for _ in range(2)]
        if outs:
            sums = [sum_in[0], sum_in[1]]
        for i, (_, _, piece, _) in enumerate(with_scales):
            sums[piece[0] == "K"] += tiles[i].astype(jnp.float32)
        if last:
            results[0][0] = sums[0][0:2]
            results[0][1] = sums[0][2:4]
            results[1][...] = sums[1][0:2]
        else:
            results[0][0] = sums[0]
            results[0][1] = sums[1]
        for c in copies:
            c.wait()

    out_shape = [EXP_OUT, KV_OUT]
    out_specs = [pl.BlockSpec(memory_space=pl.ANY)] * 2
    if last:
        out_shape += [
            jax.ShapeDtypeStruct((SLOTS, 2, LANES), jnp.float32),
            jax.ShapeDtypeStruct((2, LANES), jnp.float32),
        ]
        out_specs += [pl.BlockSpec(memory_space=VMEM)] * 2
    else:
        out_shape += [jax.ShapeDtypeStruct((2, TILE, LANES), jnp.float32)]
        out_specs += [pl.BlockSpec(memory_space=VMEM)]
    if pack:
        out_shape += [jax.ShapeDtypeStruct((total, TILE, LANES), jnp.bfloat16)]
        out_specs += [pl.BlockSpec(memory_space=pltpu.HBM)]
    first_out = 1 + len(arrays)
    return pl.pallas_call(
        kernel,
        out_shape=tuple(out_shape),
        in_specs=[pl.BlockSpec(memory_space=SMEM)]
        + [pl.BlockSpec(memory_space=pl.ANY)] * (len(arrays) + (2 if outs else 0))
        + [pl.BlockSpec(memory_space=VMEM)] * (1 if outs else 0),
        out_specs=tuple(out_specs),
        scratch_shapes=[
            pltpu.VMEM((len(with_scales), TILE, LANES), jnp.bfloat16),
            pltpu.SemaphoreType.DMA((len(with_scales),)),
            pltpu.SemaphoreType.DMA((count,)),
        ],
        input_output_aliases={first_out: 0, first_out + 1: 1} if outs else {},
        compiler_params=pltpu.CompilerParams(vmem_limit_bytes=4 * 1024 * 1024),
        cost_estimate=pl.CostEstimate(flops=0, transcendentals=0, bytes_accessed=count * 2**19),
        name="lay",
    )(place, *arrays, *(outs or []))


def after(*values):
    return lax.optimization_barrier(values)


def swap_core(v):
    return lax.ppermute(v, "c", ring(2, 1))


def swap_y(v):
    return lax.ppermute(v, "yl", ring(2, 1))


def along_x(v, k=1):
    step = (k, 4 - k)
    pairs = [(2 * x + c, 2 * ((x + step[c]) % 4) + c) for x in range(4) for c in range(2)]
    return lax.ppermute(v, ("x", "c"), pairs)


def along_z(v, k=1):
    step = (k, 4 - k)
    pairs = [(4 * c + z, 4 * c + (z + step[c]) % 4) for c in range(2) for z in range(4)]
    return lax.ppermute(v, ("c", "z"), pairs)


def per_device(
    kv_param, kv_grad, kv_mean, kv_square, exp_param, exp_grad, exp_mean, exp_square, expert_owner
):
    total = sum_over_devices(sum_of_squares(kv_grad, exp_grad))
    place = lax.axis_index(SHARD).astype(jnp.int32).reshape(1)
    kv_new, exp_new, *parts, kv_part = update(
        place,
        expert_owner,
        total,
        (kv_param, kv_grad, kv_mean, kv_square),
        (exp_param, exp_grad, exp_mean, exp_square),
    )
    parts = [parts[0]] + [along_z(parts[k], k) for k in (1, 2, 3)]
    kv_across = swap_y(kv_part)
    kv_two = jnp.stack([kv_part, kv_across])
    kv_far = [along_x(kv_two, k) for k in (1, 2, 3)]
    *parts, kv_part, kv_across, k1, k2, k3 = after(*parts, kv_part, kv_across, *kv_far)

    w0 = join_kv(place, (kv_part, kv_across, k1, k2, k3))
    p0 = join(place, parts)
    q0, p1, p3, w1, w3 = swap_y(p0), along_x(p0), along_x(p0, 3), along_z(w0), along_z(w0, 3)
    q0, p1, p3, w1, w3 = after(q0, p1, p3, w1, w3)

    b1, b3, p2 = swap_y(p1[A_T:FULL_T]), swap_y(p3[A_T:FULL_T]), along_x(p1)
    qa = q0[0:A_T]
    a1, a3 = along_x(qa), along_x(qa, 3)
    held1 = [("P", 0, False), ("P", 1, False), ("P", 3, False), ("P", 0, True)]
    held1 += [("K", 0, False), ("K", 1, False), ("K", 3, False)]
    *outs, pack1 = lay(place, list(zip([p0, p1, p3, q0, w0, w1, w3], held1)), [], pack=7)
    a1, a3, b1, b3, p2, pack1, *outs = after(a1, a3, b1, b3, p2, pack1, *outs)

    b2, a2, w2 = swap_y(p2[A_T:FULL_T]), along_x(a1), along_z(w1)
    got1, got_p2 = swap_core(pack1), swap_core(p2)
    held2 = [("A", 1, True), ("A", 3, True), ("B", 1, True), ("B", 3, True)]
    held_p2 = [("P", 2, False)]
    own = list(zip([a1, a3, b1, b3, p2], held2 + held_p2))
    *outs, pack2 = lay(place, own, [], outs, pack=4)
    a2, b2, w2, got1, got_p2, pack2, *outs = after(a2, b2, w2, got1, got_p2, pack2, *outs)

    held3 = [("A", 2, True), ("B", 2, True), ("K", 2, False)]
    own = [a2, b2, w2]
    got2 = swap_core(pack2)
    got3 = [(swap_core(v), [p]) for v, p in zip(own, held3)]
    outs = lay(place, list(zip(own, held3)), [(got1, held1), (got_p2, held_p2)], outs)
    got = [(got2, held2)] + got3
    exp_rollout, kv_rollout, exp_scales, kv_scales = lay(place, [], got, outs, last=True)
    return (
        kv_new,
        exp_new,
        kv_rollout.reshape(2, 64, BLK, BLK),
        kv_scales[:, 0:64],
        exp_rollout.reshape(SLOTS, 1, 192, BLK, BLK),
        exp_scales.reshape(SLOTS, 1, 2 * LANES)[:, :, 0:192],
    )


def solution(mesh):
    fine = Mesh(mesh.devices.reshape(4, 2, 2, 4, 2), ("x", "yl", "c", "z", "yh"))
    kv = P("yh", SHARD, None, None)
    exp = P(None, "yh", SHARD, None, None)
    return jax.shard_map(
        per_device,
        mesh=fine,
        in_specs=(kv, kv, kv, kv, exp, exp, exp, exp, P()),
        out_specs=(
            kv,
            exp,
            P("yh", None, None, None),
            P("yh", None),
            P("z", "yh", None, None, None),
            P("z", "yh", None),
        ),
        check_vma=False,
    )
```
